32 devices in a mesh: rep: 8 (over z, x), gz: 4 (over y, core).
Axes of the slice: x: 2, y: 2, z: 4, core: 2. Of those that a mesh axis runs over, the one named last changes fastest.
Arguments:
- lattice_field: float32 [48, 64, 4096], P('rep', 'gz'), may hold values from -4 to 4
- langevin_noise: float32 [2, 48, 64, 4096], P(None, 'rep', 'gz'), may hold values from -5 to 5
- masses: float32 [64, 4096], P('gz'), may hold values from -2 to 2
- counts: int32 [48], replicated, may hold values from 0 to 13, as said below
- dest_slots: int32 [48], replicated, may hold values from 0 to 47, each once
- mode_bins: int32 [64, 64, 33], P('gz'), may hold values from 0 to 15, as said below
Outputs:
- resampled: float32 [48, 64, 4096], P('rep', 'gz')
- propagator: float32 [48, 16], P('rep')
The draws below stay inside these ranges and needn't reach their ends.
Inputs may be any that keep to these rules, and one draw needn't show every extreme that they name: The counts sum to 48; in each aligned block of 6 replicas (those of one index of rep) at most 3 counts are nonzero, and exactly 3 in some block. `dest_slots`: A permutation of the 48 slots. `mode_bins`: the bin depends only on n_y^2 + n_z^2 + kx^2 with n = min(k, 64 - k), and never falls as that grows; every bin holds at least one mode.
All inputs are finite; a program needn't handle non-finite values.
Results may differ from the reference program's by a relative error of at most 0.00007.
Values sent between devices are 32-bit elements; how exact they have to be, the bound alone decides.
A program may use at most 64 MiB of HBM per device.

```python
import jax
import jax.numpy as jnp
from jax import lax

L = 64
REP_DEV = 6
SWEEPS = 2
NBINS = 16
LIVE_DEV = 3
REPLICAS = 48


def draw_counts(key, part):
    subkeys = jax.random.split(key, 4)
    blocks = REPLICAS // REP_DEV
    least = max((LIVE_DEV + 1) // 2, 1)
    live_number = jax.random.randint(subkeys[0], (blocks,), least, LIVE_DEV + 1)
    chosen = jax.random.randint(subkeys[1], (), 0, blocks)
    live_number = jnp.where(jnp.arange(blocks) == chosen, LIVE_DEV, live_number)
    scores = jax.random.randint(subkeys[2], (blocks, REP_DEV), 0, 1 << 20) * REP_DEV + jnp.arange(REP_DEV)[None, :]
    ranking = jnp.argsort(jnp.argsort(scores, axis=1), axis=1)
    alive = (ranking < live_number[:, None]).reshape(REPLICAS).astype(jnp.int32)
    total_live = jnp.sum(alive)
    live_first = jnp.argsort(1 - alive, stable=True)
    big_extra = REPLICAS // 4
    second_extra = REPLICAS // 8
    big_index = jax.random.randint(subkeys[3], (), 0, 1 << 20) % total_live
    second_index = (big_index + 1) % total_live
    remaining = REPLICAS - total_live - big_extra - second_extra
    others = total_live - 2
    turns = jnp.arange(REPLICAS)
    spots = (big_index + 2 + turns // 3 % others) % total_live
    target = live_first[spots]
    extra = (turns < remaining).astype(jnp.int32)
    spread = jnp.zeros((REPLICAS,), jnp.int32).at[target].add(extra)
    big_add = jnp.zeros((REPLICAS,), jnp.int32).at[live_first[big_index]].add(big_extra)
    second_add = jnp.zeros((REPLICAS,), jnp.int32).at[live_first[second_index]].add(second_extra)
    return (alive + spread + big_add + second_add).astype(jnp.int32)


def draw_mode_bins(key, part):
    half = L // 2
    folded = jnp.minimum(jnp.arange(L), L - jnp.arange(L))
    wave_x = jnp.arange(half + 1)
    squared = folded[:, None, None] ** 2 + folded[None, :, None] ** 2 + wave_x[None, None, :] ** 2
    reach = half * half
    offsets = jnp.sort(jax.random.randint(key, (NBINS - 1,), 0, reach - 8 * NBINS))
    edges = 8 * jnp.arange(1, NBINS) + offsets
    return jnp.sum((squared[..., None] >= edges).astype(jnp.int32), axis=-1).astype(jnp.int32)


def levels(rng, dims, cuts, low, top_value):
    gain, own = 1.0, jax.random.fold_in(rng, 6)
    for axis_at, shards_of in cuts:
        heights = jnp.exp(jax.random.uniform(jax.random.fold_in(own, axis_at), (shards_of,), jnp.float32, low / len(cuts), top_value / len(cuts)))
        gain = gain * jnp.repeat(heights, dims[axis_at] // shards_of).reshape([-1 if axis == axis_at else 1 for axis in range(len(dims))])
    return gain


def noise(stream_key, extent, scale, bound, shards=(), held_as=jnp.bfloat16):
    level = levels(stream_key, extent, shards, -0.22, 0.18) if shards else 1.0
    array = jax.random.normal(stream_key, extent, jnp.float32) * scale * level
    return jnp.minimum(jnp.maximum(array, -bound), bound).astype(held_as)


def setup_inputs(seed: int = 0) -> dict:
    streams_of = jax.random.split(jax.random.key(seed), 7)
    return {
        "lattice_field": noise(streams_of[0], (REPLICAS, L, L * L), 1.0, 4.0, ((0, 8), (1, 4)), jnp.float32),
        "langevin_noise": noise(streams_of[1], (SWEEPS, REPLICAS, L, L * L), 1.0, 5.0, ((1, 8), (2, 4)), jnp.float32),
        "masses": jnp.clip(jax.random.uniform(streams_of[2], (L, L * L), jnp.float32, -2.0, 2.0) * levels(streams_of[2], (L, L * L), ((0, 4),), -0.4, 0.0), -2.0, 2.0),
        "counts": draw_counts(jax.random.fold_in(streams_of[6], 71), 0),
        "dest_slots": jax.random.permutation(streams_of[4], REPLICAS).astype(jnp.int32),
        "mode_bins": draw_mode_bins(jax.random.fold_in(streams_of[6], 71), 0),
    }


step_size = 0.1
quartic = 0.5

def sweep(field, noise_now, masses):
    plane = jnp.roll(field, 1, axis=1) + jnp.roll(field, -1, axis=1)
    grid = field.reshape(field.shape[0], L, L, L)
    inner = jnp.roll(grid, 1, axis=2) + jnp.roll(grid, -1, axis=2) + jnp.roll(grid, 1, axis=3) + jnp.roll(grid, -1, axis=3)
    beside = plane + inner.reshape(field.shape)
    drift = 6.0 * field - beside + masses[None] * field + quartic * field * field * field
    return field - step_size * drift + jnp.sqrt(2.0 * step_size) * noise_now

def sources(counts, dest_slots):
    ends = jnp.cumsum(counts).astype(jnp.int32)
    position = jnp.argsort(dest_slots).astype(jnp.int32)
    return lax.optimization_barrier(jnp.sum((ends[None, :] <= position[:, None]).astype(jnp.int32), axis=1)).astype(jnp.int32)

def mode_weights(mode_bins):
    ordered = jnp.transpose(mode_bins, (1, 0, 2))
    wave_x = jnp.arange(L // 2 + 1)
    weight_x = jnp.where((wave_x == 0) | (wave_x == L // 2), 1.0, 2.0).astype(jnp.float32)
    onehot = (ordered[..., None] == jnp.arange(NBINS)[None, None, None, :]).astype(jnp.float32)
    return (onehot * weight_x[None, None, :, None]).reshape(-1, NBINS)

def reference(lattice_field, langevin_noise, masses, counts, dest_slots, mode_bins):
    swept = lattice_field
    for turn in range(SWEEPS):
        swept = sweep(swept, langevin_noise[turn], masses)
    source = sources(counts, dest_slots)
    resampled = jnp.take(swept, source, axis=0)
    weights = mode_weights(mode_bins)

    def one_replica(replica):
        spectrum = jnp.fft.rfftn(replica.reshape(L, L, L))
        power = jnp.real(spectrum) ** 2 + jnp.imag(spectrum) ** 2
        return jnp.dot(power.reshape(1, -1), weights, precision=lax.Precision.HIGHEST)[0]
    binned = lax.map(one_replica, resampled)
    bin_weight = lax.optimization_barrier(jnp.sum(weights, axis=0))
    propagator = binned / (float(L ** 3) * bin_weight)
    return (resampled, propagator)
```

```python
import jax
import jax.numpy as jnp
from jax import lax
from jax.sharding import PartitionSpec as P

L = 64
HALF = L // 2 + 1
SWEEPS = 2
NBINS = 16
LIVE_DEV = 3

step_size = 0.1
quartic = 0.5


def ring(axis):
    count = lax.axis_size(axis)
    forward = [(i, (i + 1) % count) for i in range(count)]
    backward = [(target, source) for source, target in forward]
    return forward, backward


def in_plane(center):
    grid = center.reshape(center.shape[0], center.shape[1], L, L)
    across = jnp.roll(grid, 1, axis=3) + jnp.roll(grid, -1, axis=3)
    return jnp.roll(center, L, axis=2) + jnp.roll(center, -L, axis=2) + across.reshape(center.shape)


def update(padded, site_masses, noise_now):
    center = padded[:, 1:-1]
    beside = padded[:, :-2] + padded[:, 2:] + in_plane(center)
    drift = 6.0 * center - beside + site_masses[None] * center + quartic * center * center * center
    return center - step_size * drift + jnp.sqrt(2.0 * step_size) * noise_now


def angle_tables(rows, columns):
    product = jnp.arange(rows)[:, None] * jnp.arange(columns)[None, :] % L
    theta = 2.0 * jnp.pi / L * product.astype(jnp.float32)
    return (jnp.cos(theta), jnp.sin(theta))


def binned_power(slabs, mode_bins):
    exact = lax.Precision.HIGH
    cos_half, sin_half = angle_tables(L, HALF)
    cos_full, sin_full = angle_tables(L, L)
    along_x = jnp.concatenate([cos_half, -sin_half], axis=1)
    count, depth = (slabs.shape[0], slabs.shape[1])
    grid = slabs.reshape(count, depth, L, L)
    first = jnp.einsum("nzyx,xk->nzyk", grid, along_x, precision=exact)
    both = jnp.concatenate([cos_full, sin_full], axis=0)
    second = jnp.einsum("qy,nzyk->qnzk", both, first, precision=exact)
    cos_part, sin_part = second[:L], second[L:]
    real_y = cos_part[..., :HALF] + sin_part[..., HALF:]
    imag_y = cos_part[..., HALF:] - sin_part[..., :HALF]
    merged = jnp.concatenate([real_y, imag_y], axis=3)
    pencil = lax.all_to_all(merged, "gz", split_axis=0, concat_axis=2, tiled=True)
    third = jnp.einsum("pz,qnzk->pnqk", both, pencil, precision=exact)
    cos_part, sin_part = third[:L], third[L:]
    real_z = cos_part[..., :HALF] + sin_part[..., HALF:]
    imag_z = cos_part[..., HALF:] - sin_part[..., :HALF]
    wave_x = jnp.arange(HALF)
    weight_x = jnp.where((wave_x == 0) | (wave_x == L // 2), 1.0, 2.0).astype(jnp.float32)
    power = (real_z * real_z + imag_z * imag_z) * weight_x
    ordered = jnp.transpose(mode_bins, (1, 0, 2))
    hit = ordered[None] == jnp.arange(NBINS)[:, None, None, None]
    binned = jnp.sum(jnp.where(hit[:, :, None], power[None], 0.0), axis=(1, 3, 4))
    weight = jnp.sum(jnp.where(hit, weight_x, 0.0), axis=(1, 2, 3))
    return jnp.concatenate([binned, weight[:, None]], axis=1).T


def local(lattice_field, langevin_noise, masses, counts, dest_slots, mode_bins):
    local_count = lattice_field.shape[0]
    blocks = counts.shape[0] // local_count
    me = lax.axis_index("rep")
    alive = (counts > 0).astype(jnp.int32).reshape(blocks, local_count)
    rank = jnp.cumsum(alive, axis=1) - alive
    place = (jnp.arange(blocks)[:, None] * LIVE_DEV + rank).reshape(-1)
    mine_alive = lax.dynamic_index_in_dim(alive, me, 0, keepdims=False)
    mine_rank = lax.dynamic_index_in_dim(rank, me, 0, keepdims=False)
    turns = jnp.arange(LIVE_DEV)
    pick = (mine_alive[None, :] > 0) & (mine_rank[None, :] == turns[:, None])
    live = jnp.sum(pick.astype(jnp.int32) * jnp.arange(local_count)[None, :], axis=1)

    def take(array, axis):
        return jnp.concatenate(
            [lax.dynamic_slice_in_dim(array, live[i], 1, axis=axis) for i in range(LIVE_DEV)], axis=axis
        )

    field = take(lattice_field, 0)
    noise = take(langevin_noise, 1)
    forward, backward = ring("gz")
    swept = field
    for turn in range(SWEEPS):
        low = lax.ppermute(swept[:, -1:], "gz", forward)
        high = lax.ppermute(swept[:, :1], "gz", backward)
        swept = update(jnp.concatenate([low, swept, high], axis=1), masses, noise[turn])
    piece = lax.all_gather(swept, "rep", axis=0, tiled=True)

    ends = jnp.cumsum(counts)
    owner = jnp.sum((ends[None, :] <= dest_position(dest_slots)[:, None]).astype(jnp.int32), axis=1)
    source = jnp.sum(jnp.where(owner[:, None] == jnp.arange(counts.shape[0])[None], place[None], 0), axis=1)
    mine = lax.dynamic_slice_in_dim(source, me * local_count, local_count)
    resampled = jnp.concatenate(
        [lax.dynamic_slice_in_dim(piece, mine[i], 1, axis=0) for i in range(local_count)], axis=0
    )

    total = lax.psum(binned_power(swept, mode_bins), "gz")
    propagators = total[:LIVE_DEV] / (float(L**3) * total[LIVE_DEV:])
    everyone = lax.all_gather(propagators, "rep", axis=0, tiled=True)
    propagator = jnp.take(everyone, mine, axis=0)
    return (resampled, propagator)


def dest_position(dest_slots):
    slots = jnp.arange(dest_slots.shape[0])
    return jnp.sum(jnp.where(dest_slots[None, :] == slots[:, None], slots[None, :], 0), axis=1)


def solution(mesh):
    in_specs = (
        P("rep", "gz", None),
        P(None, "rep", "gz", None),
        P("gz", None),
        P(),
        P(),
        P("gz", None, None),
    )
    out_specs = (P("rep", "gz", None), P("rep", None))
    return jax.shard_map(local, mesh=mesh, in_specs=in_specs, out_specs=out_specs, check_vma=False)
```

```python
import functools

import jax
import jax.numpy as jnp
import numpy as np
from jax import lax
from jax.experimental import pallas as pl
from jax.experimental.pallas import tpu as pltpu
from jax.sharding import PartitionSpec as P

L = 64
HALF = L // 2 + 1
SWEEPS = 2
NBINS = 16
LIVE_DEV = 3
COLUMNS = 2
PIECES = 2 * LIVE_DEV
CHUNKS = L * L // 128

step_size = 0.1
quartic = 0.5
kick = float(np.sqrt(np.float32(2.0 * step_size)))
MESH = pl.DeviceIdType.MESH


def tables():
    angle = 2.0 * np.pi / L * (np.outer(np.arange(L), np.arange(L)) % L)
    cos, sin = np.cos(angle), np.sin(angle)
    along_x = np.zeros((128, 512))
    for parity in range(2):
        rows = slice(64 * parity, 64 * parity + 64)
        at = 128 * parity
        along_x[rows, at : at + HALF] = cos[:, :HALF]
        along_x[rows, at + 64 : at + 64 + HALF] = -sin[:, :HALF]
        at = 256 + 128 * parity
        along_x[rows, at : at + HALF] = -sin[:, :HALF]
        along_x[rows, at + 64 : at + 64 + HALF] = -cos[:, :HALF]
    along_y = np.concatenate([cos[:, 0::2], cos[:, 1::2], sin[:, 0::2], sin[:, 1::2]], axis=1)
    along_z = np.concatenate([cos, sin], axis=1)

    def halves(table):
        table = table.astype(np.float32)
        high = table.astype(jnp.bfloat16)
        return np.stack([high, (table - high.astype(np.float32)).astype(jnp.bfloat16)])

    return halves(along_x), halves(along_y), halves(along_z)


def split(value):
    high = value.astype(jnp.bfloat16)
    return high, (value - high.astype(jnp.float32)).astype(jnp.bfloat16)


def dot(left, right):
    def one(a, b):
        return jnp.dot(a, b, preferred_element_type=jnp.float32)

    return one(left[0], right[0]) + (one(left[0], right[1]) + one(left[1], right[0]))


def kernel(reps, gzs, rep_dev, counts, dest, field, noise, masses, bins_in, tx, ty, tz, out, prop, *scratch):
    (
        swept, gathered, edge_out, edge_in, work, sent, modes, bins, acc, part, props, own_part, own_prop,
        up_sem, down_sem, own_x_sem, up_x_sem, down_x_sem, recv_sem,
        edge_send, edge_recv, mode_send, mode_recv, part_send, part_recv, prop_send, prop_recv,
    ) = scratch
    depth = field.shape[1]
    per = L // gzs
    levels = reps // COLUMNS
    me, ring = lax.axis_index("rep"), lax.axis_index("gz")
    z, x = me // COLUMNS, me % COLUMNS
    mate = z * COLUMNS + (1 - x)

    barrier = pltpu.get_barrier_semaphore()

    def greet(turn, carry):
        pl.semaphore_signal(barrier, inc=1, device_id=(me, (ring + turn) % gzs), device_id_type=MESH)
        return carry

    def greet_rep(turn, carry):
        pl.semaphore_signal(barrier, inc=1, device_id=((me + turn) % reps, ring), device_id_type=MESH)
        return carry

    lax.fori_loop(1, gzs, greet, 0)
    lax.fori_loop(1, reps, greet_rep, 0)

    live = [jnp.int32(0)] * LIVE_DEV
    rank = jnp.int32(0)
    for i in range(rep_dev):
        alive = counts[me * rep_dev + i] > 0
        live = [jnp.where(alive & (rank == k), i, live[k]) for k in range(LIVE_DEV)]
        rank = rank + alive.astype(jnp.int32)

    for k in range(LIVE_DEV):
        swept[k, 8 : 8 + depth, :] = field[live[k]]
    pl.semaphore_wait(barrier, gzs - 1 + reps - 1)

    lane = lax.broadcasted_iota(jnp.int32, (depth, 128), 1)
    first_x, last_x, even_y = lane % 64 == 0, lane % 64 == 63, lane < 64

    def edge_copy(turn, side):
        target = (ring + 1) % gzs if side == 0 else (ring + gzs - 1) % gzs
        return pltpu.make_async_remote_copy(
            src_ref=edge_out.at[turn, side], dst_ref=edge_in.at[turn, side],
            send_sem=edge_send.at[turn, side], recv_sem=edge_recv.at[turn, side],
            device_id=(me, target), device_id_type=MESH,
        )

    def piece(owner, index):
        return gathered.at[owner * LIVE_DEV + index // 2, index % 2]

    def send(owner, index, sem, target):
        ref = piece(owner, index)
        return pltpu.make_async_remote_copy(
            src_ref=ref, dst_ref=ref, send_sem=sem, recv_sem=recv_sem.at[owner * PIECES + index],
            device_id=(target, ring), device_id_type=MESH,
        )

    for turn in range(SWEEPS):
        for k in range(LIVE_DEV):
            edge_out[turn, 0, k] = swept[turn * LIVE_DEV + k, 8 + depth - 1 : 8 + depth, :]
            edge_out[turn, 1, k] = swept[turn * LIVE_DEV + k, 8:9, :]
        for side in range(2):
            edge_copy(turn, side).start()
        for side in range(2):
            edge_copy(turn, side).wait()
        for k in range(LIVE_DEV):
            swept[turn * LIVE_DEV + k, 7:8, :] = edge_in[turn, 0, k]
            swept[turn * LIVE_DEV + k, 8 + depth : 9 + depth, :] = edge_in[turn, 1, k]
        for k in range(LIVE_DEV):
            from_at, to_at = turn * LIVE_DEV + k, (turn + 1) * LIVE_DEV + k

            def block(j, carry):
                def lanes(at):
                    return pl.ds(pl.multiple_of(at % CHUNKS * 128, 128), 128)

                here = lanes(j)
                center = swept[from_at, 8 : 8 + depth, here]
                before = pltpu.roll(swept[from_at, 8 : 8 + depth, lanes(j + CHUNKS - 1)], 64, 1)
                after = pltpu.roll(swept[from_at, 8 : 8 + depth, lanes(j + 1)], 64, 1)
                beside = swept[from_at, 7 : 7 + depth, here] + swept[from_at, 9 : 9 + depth, here]
                beside += pltpu.roll(center, 64, 1) + jnp.where(even_y, before, after)
                beside += jnp.where(first_x, pltpu.roll(center, 65, 1), pltpu.roll(center, 1, 1))
                beside += jnp.where(last_x, pltpu.roll(center, 63, 1), pltpu.roll(center, 127, 1))
                drift = 6.0 * center - beside + masses[:, here] * center + quartic * center * center * center
                fresh = center - step_size * drift + kick * noise[turn, live[k], :, here]
                if turn + 1 < SWEEPS:
                    swept[to_at, 8 : 8 + depth, here] = fresh
                else:
                    at = pl.ds(pl.multiple_of(j % (CHUNKS // 2) * 128, 128), 128)
                    gathered[me * LIVE_DEV + k, j // (CHUNKS // 2), :, at] = fresh
                    work[k, pl.ds(j, depth, stride=CHUNKS), :] = fresh
                return carry

            lax.fori_loop(0, CHUNKS, block, 0, unroll=4)

    for index in range(PIECES):
        send(me, index, own_x_sem.at[index], mate).start()

        @pl.when(z + 1 < levels)
        def _():
            send(me, index, up_sem.at[index], me + COLUMNS).start()

        @pl.when(z > 0)
        def _():
            send(me, index, down_sem.at[index], me - COLUMNS).start()

    send(mate, 0, own_x_sem.at[0], mate).wait_recv()

    @pl.when(z + 1 < levels)
    def _():
        send(mate, 0, up_sem.at[PIECES], me + COLUMNS).start()

    @pl.when(z > 0)
    def _():
        send(mate, 0, down_sem.at[PIECES], me - COLUMNS).start()

    def forward(t, at):
        foreign = (at == PIECES).astype(jnp.int32)
        index = at - PIECES * foreign
        column = x + foreign * (1 - 2 * x)
        for sign, sem, x_sem, edge in ((1, up_sem, up_x_sem, levels - 1), (-1, down_sem, down_x_sem, 0)):
            origin = z - sign * t
            owner = origin * COLUMNS + column
            before = (origin + sign) * COLUMNS + column

            @pl.when((origin >= 0) & (origin < levels))
            def _():
                send(owner, index, sem.at[at], mate).wait_recv()

            @pl.when((origin + sign >= 0) & (origin + sign < levels) & (z != edge))
            def _():
                send(before, index, sem.at[at], me + sign * COLUMNS).wait_send()

            @pl.when((origin >= 0) & (origin < levels) & (z != edge))
            def _():
                send(owner, index, sem.at[at], me + sign * COLUMNS).start()

            @pl.when((t > 1) & (origin + sign >= 0) & (origin + sign < levels) & (at < PIECES) & (at > 0))
            def _():
                send(before, index, x_sem.at[index], mate).wait_send()

            @pl.when((origin >= 0) & (origin < levels) & (at < PIECES) & (at > 0))
            def _():
                send(owner, index, x_sem.at[index], mate).start()

    half_depth = depth // 2

    def planes(unit):
        k, part_at = unit // 2, unit % 2
        rows = half_depth * CHUNKS
        value = work[k, pl.ds(pl.multiple_of(part_at * rows, rows), rows), :]
        first = dot(split(value), (tx[0], tx[1]))
        for pair in range(half_depth // 2):
            stacked = []
            for plane in (2 * pair, 2 * pair + 1):
                mine = first[plane * CHUNKS : (plane + 1) * CHUNKS]
                stacked.append(jnp.concatenate([mine[:, 128 * c : 128 * c + 128] for c in range(4)], axis=0))
            second = dot((ty[0], ty[1]), split(jnp.concatenate(stacked, axis=1)))
            for d in range(gzs):
                rows = second[d * per : (d + 1) * per]
                at = part_at * half_depth + 2 * pair
                sent[k, d, at] = rows[:, :128]
                sent[k, d, at + 1] = rows[:, 128:]

    def mode_copy(k, turn, source):
        target = (ring + turn) % gzs
        return pltpu.make_async_remote_copy(
            src_ref=sent.at[k, target],
            dst_ref=modes.at[k, pl.ds(source * depth, depth)],
            send_sem=mode_send.at[k * gzs + turn],
            recv_sem=mode_recv.at[k * gzs + turn],
            device_id=(me, target), device_id_type=MESH,
        )

    def send_modes(k):

        def one(turn, carry):
            mode_copy(k, turn, ring).start()
            return carry

        lax.fori_loop(1, gzs, one, 0)

    def early(at, carry):
        forward(1, at)

        @pl.when(at < PIECES)
        def _():
            planes(at)

        return carry

    lax.fori_loop(0, PIECES + 1, early, 0)
    for k in range(LIVE_DEV):
        send_modes(k)

    bins[...] = jnp.full(bins.shape, -1, jnp.int32)
    for q in range(per):
        bins[q, :, 0:HALF] = bins_in[q]
        bins[q, :, 64 : 64 + HALF] = bins_in[q]
    acc[...] = jnp.zeros(acc.shape, jnp.float32)
    wide = lax.broadcasted_iota(jnp.int32, (L, 128), 1)
    wave_x = wide % 64
    weight = jnp.where((wave_x == 0) | (wave_x == L // 2), 1.0, 2.0).astype(jnp.float32)
    sign_of = jnp.where(wide < 64, 1.0, -1.0).astype(jnp.float32)
    real_weight = jnp.where(wide < 64, weight, 0.0)

    def add_bins(k, q, value):
        here = bins[q]
        for b in range(NBINS):
            taken = jnp.where(here == b, value, 0.0)
            acc[k, b] += jnp.sum(taken.reshape(L // 8, 8, 128), axis=0)

    def weigh(q, carry):
        add_bins(LIVE_DEV, q, real_weight)
        return carry

    lax.fori_loop(0, per, weigh, 0)

    def pair_modes(k, pair):
        stacked = []
        for q in (2 * pair, 2 * pair + 1):
            mine = modes[k, :, q, :]
            turned = pltpu.roll(mine, 64, 1) * sign_of
            stacked.append(jnp.concatenate([mine, turned], axis=0))
        third = dot((tz[0], tz[1]), split(jnp.concatenate(stacked, axis=1)))
        for n in range(2):
            value = third[:, 128 * n : 128 * n + 128]
            add_bins(k, 2 * pair + n, value * value * weight)

    def middle(at, carry):
        forward(2, at)

        @pl.when(at < PIECES)
        def _():
            def go(pair, c):
                pair_modes(at // 2, at % 2 * (per // 4) + pair)
                return c

            lax.fori_loop(0, per // 4, go, 0)

        return carry

    for k in range(LIVE_DEV):

        def arrive(turn, c):
            mode_copy(k, turn, (ring + gzs - turn) % gzs).wait_recv()
            mode_copy(k, turn, ring).wait_send()
            return c

        lax.fori_loop(1, gzs, arrive, 0)
    for k in range(LIVE_DEV):
        modes[k, pl.ds(ring * depth, depth)] = sent[k, ring]
    lax.fori_loop(0, PIECES + 1, middle, 0)

    at_lane = lax.broadcasted_iota(jnp.int32, (NBINS, 128), 1)
    at_row = lax.broadcasted_iota(jnp.int32, (NBINS, 128), 0)
    rows = []
    for k in range(LIVE_DEV + 1):
        summed = jnp.sum(jnp.sum(acc[k], axis=1), axis=1, keepdims=True)
        rows.append(jnp.sum(jnp.where(at_lane == at_row, summed, 0.0), axis=0, keepdims=True))
    own_part[...] = jnp.concatenate(rows + [jnp.zeros((8 - LIVE_DEV - 1, 128), jnp.float32)], axis=0)

    def part_copy(turn, to):
        return pltpu.make_async_remote_copy(
            src_ref=own_part, dst_ref=part.at[to],
            send_sem=part_send.at[turn], recv_sem=part_recv.at[turn],
            device_id=(me, (ring + turn) % gzs), device_id_type=MESH,
        )

    def part_start(turn, carry):
        part_copy(turn, ring).start()
        return carry

    def part_wait(turn, carry):
        part_copy(turn, (ring + gzs - turn) % gzs).wait_recv()
        part_copy(turn, ring).wait_send()
        return carry

    lax.fori_loop(1, gzs, part_start, 0)

    total = jnp.int32(0)
    slots = [jnp.int32(0)] * rep_dev

    def position_of(p, found):
        slot = dest[p]
        return tuple(jnp.where(slot == me * rep_dev + j, p, found[j]) for j in range(rep_dev))

    found = lax.fori_loop(0, reps * rep_dev, position_of, tuple(slots))

    def look(i, state):
        total, rank, owners, ranks = state
        number = counts[i]
        rank = jnp.where(i % rep_dev == 0, 0, rank)
        ends = total + number
        hits = [(found[j] >= total) & (found[j] < ends) for j in range(rep_dev)]
        owners = tuple(jnp.where(hits[j], i // rep_dev, owners[j]) for j in range(rep_dev))
        ranks = tuple(jnp.where(hits[j], rank, ranks[j]) for j in range(rep_dev))
        return ends, rank + (number > 0).astype(jnp.int32), owners, ranks

    _, _, owners, ranks = lax.fori_loop(
        0, reps * rep_dev, look, (total, jnp.int32(0), tuple(slots), tuple(slots))
    )

    lax.fori_loop(1, gzs, part_wait, 0)
    part[ring] = own_part[...]
    binned = jnp.sum(part[...], axis=0)
    whole = binned[LIVE_DEV : LIVE_DEV + 1]
    used = lax.broadcasted_iota(jnp.int32, (8, 128), 1) < NBINS
    own_prop[...] = jnp.where(used, binned / jnp.where(used, float(L**3) * whole, 1.0), 0.0)

    def prop_copy(turn, to):
        return pltpu.make_async_remote_copy(
            src_ref=own_prop, dst_ref=props.at[to],
            send_sem=prop_send.at[turn], recv_sem=prop_recv.at[turn],
            device_id=((me + turn) % reps, ring), device_id_type=MESH,
        )

    def prop_start(turn, carry):
        prop_copy(turn, me).start()
        return carry

    def prop_wait(turn, carry):
        prop_copy(turn, (me + reps - turn) % reps).wait_recv()
        prop_copy(turn, me).wait_send()
        return carry

    lax.fori_loop(1, reps, prop_start, 0)

    def late(step, carry):
        forward(3 + step // (PIECES + 1), step % (PIECES + 1))
        return carry

    lax.fori_loop(0, (levels - 3) * (PIECES + 1), late, 0)

    lax.fori_loop(1, reps, prop_wait, 0)
    props[me] = own_prop[...]
    for j in range(rep_dev):
        prop[j : j + 1, :] = props[owners[j], pl.ds(ranks[j], 1), :][:, :NBINS]

    def from_mate(step, carry):
        origin, index = step // PIECES, step % PIECES

        @pl.when(index > 0)
        def _():
            send(origin * COLUMNS + 1 - x, index, own_x_sem.at[index], mate).wait_recv()

        return carry

    lax.fori_loop(0, levels * PIECES, from_mate, 0)

    half = CHUNKS * 64
    for j in range(rep_dev):
        for h in range(2):
            out[j, :, half * h : half * h + half] = gathered[owners[j] * LIVE_DEV + ranks[j], h]

    def drain(index, carry):
        send(me, index, own_x_sem.at[index], mate).wait_send()
        for origin, x_sem, last in ((0, up_x_sem, levels - 1), (levels - 1, down_x_sem, 0)):

            @pl.when((z == last) & (index > 0))
            def _():
                send(origin * COLUMNS + x, index, x_sem.at[index], mate).wait_send()

        return carry

    lax.fori_loop(0, PIECES, drain, 0)


def local(lattice_field, langevin_noise, masses, counts, dest_slots, mode_bins):
    rep_dev, depth, sites = lattice_field.shape
    reps, gzs = lax.axis_size("rep"), lax.axis_size("gz")
    per = L // gzs
    levels = reps // COLUMNS
    assert levels >= 4
    f32, dma = jnp.float32, pltpu.SemaphoreType.DMA
    scratch = [
        pltpu.VMEM((SWEEPS * LIVE_DEV, depth + 16, sites), f32),
        pltpu.VMEM((reps * LIVE_DEV, 2, depth, sites // 2), f32),
        pltpu.VMEM((SWEEPS, 2, LIVE_DEV, 1, sites), f32),
        pltpu.VMEM((SWEEPS, 2, LIVE_DEV, 1, sites), f32),
        pltpu.VMEM((LIVE_DEV, depth * CHUNKS, 128), f32),
        pltpu.VMEM((LIVE_DEV, gzs, depth, per, 128), f32),
        pltpu.VMEM((LIVE_DEV, L, per, 128), f32),
        pltpu.VMEM((per, L, 128), jnp.int32),
        pltpu.VMEM((LIVE_DEV + 1, NBINS, 8, 128), f32),
        pltpu.VMEM((gzs, 8, 128), f32),
        pltpu.VMEM((reps, 8, 128), f32),
        pltpu.VMEM((8, 128), f32),
        pltpu.VMEM((8, 128), f32),
        dma((PIECES + 1,)),
        dma((PIECES + 1,)),
        dma((PIECES,)),
        dma((PIECES,)),
        dma((PIECES,)),
        dma((reps * PIECES,)),
        dma((SWEEPS, 2)),
        dma((SWEEPS, 2)),
        dma((LIVE_DEV * gzs,)),
        dma((LIVE_DEV * gzs,)),
        dma((gzs,)),
        dma((gzs,)),
        dma((reps,)),
        dma((reps,)),
    ]
    smem = pl.BlockSpec(memory_space=pltpu.SMEM)
    vmem = pl.BlockSpec(memory_space=pltpu.VMEM)
    return pl.pallas_call(
        functools.partial(kernel, reps, gzs, rep_dev),
        out_shape=(
            jax.ShapeDtypeStruct(lattice_field.shape, f32),
            jax.ShapeDtypeStruct((rep_dev, NBINS), f32),
        ),
        in_specs=[smem, smem] + [vmem] * 7,
        out_specs=(vmem, vmem),
        scratch_shapes=scratch,
        compiler_params=pltpu.CompilerParams(
            collective_id=0, has_side_effects=True, vmem_limit_bytes=56 * 1024 * 1024
        ),
    )(counts, dest_slots, lattice_field, langevin_noise, masses, mode_bins, *map(jnp.asarray, tables()))


def solution(mesh):
    in_specs = (
        P("rep", "gz", None),
        P(None, "rep", "gz", None),
        P("gz", None),
        P(),
        P(),
        P("gz", None, None),
    )
    out_specs = (P("rep", "gz", None), P("rep", None))
    return jax.shard_map(local, mesh=mesh, in_specs=in_specs, out_specs=out_specs, check_vma=False)
```

```python
import functools

import jax
import jax.numpy as jnp
import numpy as np
from jax import lax
from jax.experimental import pallas as pl
from jax.experimental.pallas import tpu as pltpu
from jax.sharding import PartitionSpec as P

L = 64
HALF = L // 2 + 1
SWEEPS = 2
NBINS = 16
LIVE_DEV = 3
COLUMNS = 2
PIECES = 2 * LIVE_DEV
CHUNKS = L * L // 128

step_size = 0.1
quartic = 0.5
kick = float(np.sqrt(np.float32(2.0 * step_size)))
MESH = pl.DeviceIdType.MESH


def tables():
    angle = 2.0 * np.pi / L * (np.outer(np.arange(L), np.arange(L)) % L)
    cos, sin = np.cos(angle), np.sin(angle)
    along_x = np.zeros((128, 512))
    for parity in range(2):
        rows = slice(64 * parity, 64 * parity + 64)
        at = 128 * parity
        along_x[rows, at : at + HALF] = cos[:, :HALF]
        along_x[rows, at + 64 : at + 64 + HALF] = -sin[:, :HALF]
        at = 256 + 128 * parity
        along_x[rows, at : at + HALF] = -sin[:, :HALF]
        along_x[rows, at + 64 : at + 64 + HALF] = -cos[:, :HALF]
    along_y = np.concatenate([cos[:, 0::2], cos[:, 1::2], sin[:, 0::2], sin[:, 1::2]], axis=1)
    along_z = np.concatenate([cos, sin], axis=1)

    def halves(table):
        table = table.astype(np.float32)
        high = table.astype(jnp.bfloat16)
        return np.stack([high, (table - high.astype(np.float32)).astype(jnp.bfloat16)])

    return halves(along_x), halves(along_y), halves(along_z)


def split(value):
    high = value.astype(jnp.bfloat16)
    return high, (value - high.astype(jnp.float32)).astype(jnp.bfloat16)


def dot(left, right):
    def one(a, b):
        return jnp.dot(a, b, preferred_element_type=jnp.float32)

    return one(left[0], right[0]) + (one(left[0], right[1]) + one(left[1], right[0]))


def kernel(reps, gzs, rep_dev, counts, dest, field, noise, masses, bins_in, tx, ty, tz, out, prop, *scratch):
    (
        swept, gathered, edge_out, edge_in, work, sent0, sent1, sent2, modes0, modes1, modes2, bins, acc, part, props, own_part, own_prop,
        up_sem, down_sem, own_x_sem, up_x_sem, down_x_sem, recv_sem,
        edge_send, edge_recv, mode_send, mode_recv, part_send, part_recv, prop_send, prop_recv,
    ) = scratch
    sent, modes = (sent0, sent1, sent2), (modes0, modes1, modes2)
    depth = field.shape[1]
    per = L // gzs
    levels = reps // COLUMNS
    me, ring = lax.axis_index("rep"), lax.axis_index("gz")
    z, x = me // COLUMNS, me % COLUMNS
    mate = z * COLUMNS + (1 - x)

    barrier = pltpu.get_barrier_semaphore()

    def greet(turn, carry):
        pl.semaphore_signal(barrier, inc=1, device_id=(me, (ring + turn) % gzs), device_id_type=MESH)
        return carry

    def greet_rep(turn, carry):
        pl.semaphore_signal(barrier, inc=1, device_id=((me + turn) % reps, ring), device_id_type=MESH)
        return carry

    lax.fori_loop(1, gzs, greet, 0)
    lax.fori_loop(1, reps, greet_rep, 0)

    live = [jnp.int32(0)] * LIVE_DEV
    rank = jnp.int32(0)
    for i in range(rep_dev):
        alive = counts[me * rep_dev + i] > 0
        live = [jnp.where(alive & (rank == k), i, live[k]) for k in range(LIVE_DEV)]
        rank = rank + alive.astype(jnp.int32)

    lane = lax.broadcasted_iota(jnp.int32, (depth, 128), 1)
    first_x, last_x, even_y = lane % 64 == 0, lane % 64 == 63, lane < 64

    def edge_copy(turn, side, k):
        target = (ring + 1) % gzs if side == 0 else (ring + gzs - 1) % gzs
        return pltpu.make_async_remote_copy(
            src_ref=edge_out.at[turn, side, k], dst_ref=edge_in.at[turn, side, k],
            send_sem=edge_send.at[turn, side, k], recv_sem=edge_recv.at[turn, side, k],
            device_id=(me, target), device_id_type=MESH,
        )

    def edge_rows(turn, k):
        edge_out[turn, 0, k] = swept[turn * LIVE_DEV + k, 8 + depth - 1 : 8 + depth, :]
        edge_out[turn, 1, k] = swept[turn * LIVE_DEV + k, 8:9, :]

    def edge_start(turn, k):
        for side in range(2):
            edge_copy(turn, side, k).start()

    def edge_wait(turn, k):
        for side in range(2):
            edge_copy(turn, side, k).wait()
        swept[turn * LIVE_DEV + k, 7:8, :] = edge_in[turn, 0, k]
        swept[turn * LIVE_DEV + k, 8 + depth : 9 + depth, :] = edge_in[turn, 1, k]

    def piece(owner, index):
        return gathered.at[owner * LIVE_DEV + index // 2, index % 2]

    def send(owner, index, sem, target):
        ref = piece(owner, index)
        return pltpu.make_async_remote_copy(
            src_ref=ref, dst_ref=ref, send_sem=sem, recv_sem=recv_sem.at[owner * PIECES + index],
            device_id=(target, ring), device_id_type=MESH,
        )

    for k in range(LIVE_DEV):
        swept[k, 8 : 8 + depth, :] = field[live[k]]
        edge_rows(0, k)
    pl.semaphore_wait(barrier, gzs - 1 + reps - 1)
    for k in range(LIVE_DEV):
        edge_start(0, k)

    bins[...] = jnp.full(bins.shape, -1, jnp.int32)
    for q in range(per):
        bins[q, :, 0:HALF] = bins_in[q]
        bins[q, :, 64 : 64 + HALF] = bins_in[q]
    acc[...] = jnp.zeros(acc.shape, jnp.float32)
    wide = lax.broadcasted_iota(jnp.int32, (L, 128), 1)
    wave_x = wide % 64
    weight = jnp.where((wave_x == 0) | (wave_x == L // 2), 1.0, 2.0).astype(jnp.float32)
    sign_of = jnp.where(wide < 64, 1.0, -1.0).astype(jnp.float32)
    real_weight = jnp.where(wide < 64, weight, 0.0)

    def add_bins(k, q, value):
        here = bins[q]
        for b in range(NBINS):
            taken = jnp.where(here == b, value, 0.0)
            acc[k, b] += jnp.sum(taken.reshape(L // 8, 8, 128), axis=0)

    def weigh(q, carry):
        add_bins(LIVE_DEV, q, real_weight)
        return carry

    lax.fori_loop(0, per, weigh, 0)

    for turn in range(SWEEPS):
        for k in range(LIVE_DEV):
            edge_wait(turn, k)
            from_at, to_at = turn * LIVE_DEV + k, (turn + 1) * LIVE_DEV + k

            def block(j, carry):
                def lanes(at):
                    return pl.ds(pl.multiple_of(at % CHUNKS * 128, 128), 128)

                here = lanes(j)
                center = swept[from_at, 8 : 8 + depth, here]
                before = pltpu.roll(swept[from_at, 8 : 8 + depth, lanes(j + CHUNKS - 1)], 64, 1)
                after = pltpu.roll(swept[from_at, 8 : 8 + depth, lanes(j + 1)], 64, 1)
                beside = swept[from_at, 7 : 7 + depth, here] + swept[from_at, 9 : 9 + depth, here]
                beside += pltpu.roll(center, 64, 1) + jnp.where(even_y, before, after)
                beside += jnp.where(first_x, pltpu.roll(center, 65, 1), pltpu.roll(center, 1, 1))
                beside += jnp.where(last_x, pltpu.roll(center, 63, 1), pltpu.roll(center, 127, 1))
                drift = 6.0 * center - beside + masses[:, here] * center + quartic * center * center * center
                fresh = center - step_size * drift + kick * noise[turn, live[k], :, here]
                if turn + 1 < SWEEPS:
                    swept[to_at, 8 : 8 + depth, here] = fresh
                else:
                    at = pl.ds(pl.multiple_of(j % (CHUNKS // 2) * 128, 128), 128)
                    gathered[me * LIVE_DEV + k, j // (CHUNKS // 2), :, at] = fresh
                    work[k, pl.ds(j, depth, stride=CHUNKS), :] = fresh
                return carry

            lax.fori_loop(0, CHUNKS, block, 0, unroll=8)
            if turn + 1 < SWEEPS:
                edge_rows(turn + 1, k)
                edge_start(turn + 1, k)
                continue
            for index in (2 * k, 2 * k + 1):
                send(me, index, own_x_sem.at[index], mate).start()

                @pl.when(z + 1 < levels)
                def _():
                    send(me, index, up_sem.at[index], me + COLUMNS).start()

                @pl.when(z > 0)
                def _():
                    send(me, index, down_sem.at[index], me - COLUMNS).start()

    send(mate, 0, own_x_sem.at[0], mate).wait_recv()

    @pl.when(z + 1 < levels)
    def _():
        send(mate, 0, up_sem.at[PIECES], me + COLUMNS).start()

    @pl.when(z > 0)
    def _():
        send(mate, 0, down_sem.at[PIECES], me - COLUMNS).start()

    def forward(t, at):
        foreign = (at == PIECES).astype(jnp.int32)
        index = at - PIECES * foreign
        column = x + foreign * (1 - 2 * x)
        for sign, sem, x_sem, edge in ((1, up_sem, up_x_sem, levels - 1), (-1, down_sem, down_x_sem, 0)):
            origin = z - sign * t
            owner = origin * COLUMNS + column
            before = (origin + sign) * COLUMNS + column

            @pl.when((origin >= 0) & (origin < levels))
            def _():
                send(owner, index, sem.at[at], mate).wait_recv()

            @pl.when((origin + sign >= 0) & (origin + sign < levels) & (z != edge))
            def _():
                send(before, index, sem.at[at], me + sign * COLUMNS).wait_send()

            @pl.when((origin >= 0) & (origin < levels) & (z != edge))
            def _():
                send(owner, index, sem.at[at], me + sign * COLUMNS).start()

            @pl.when((t > 1) & (origin + sign >= 0) & (origin + sign < levels) & (at < PIECES) & (at > 0))
            def _():
                send(before, index, x_sem.at[index], mate).wait_send()

            @pl.when((origin >= 0) & (origin < levels) & (at < PIECES) & (at > 0))
            def _():
                send(owner, index, x_sem.at[index], mate).start()

    half_depth = depth // 2

    def planes(k, part_at):
        rows = half_depth * CHUNKS
        value = work[k, pl.ds(pl.multiple_of(part_at * rows, rows), rows), :]
        first = dot(split(value), (tx[0], tx[1]))
        for pair in range(half_depth // 2):
            stacked = []
            for plane in (2 * pair, 2 * pair + 1):
                mine = first[plane * CHUNKS : (plane + 1) * CHUNKS]
                stacked.append(jnp.concatenate([mine[:, 128 * c : 128 * c + 128] for c in range(4)], axis=0))
            second = dot((ty[0], ty[1]), split(jnp.concatenate(stacked, axis=1)))
            for d in range(gzs):
                rows = second[d * per : (d + 1) * per]
                at = part_at * half_depth + 2 * pair
                sent[k][d, at] = rows[:, :128]
                sent[k][d, at + 1] = rows[:, 128:]

    def mode_copy(k, turn, source):
        target = (ring + turn) % gzs
        return pltpu.make_async_remote_copy(
            src_ref=sent[k].at[target],
            dst_ref=modes[k].at[pl.ds(source * depth, depth)],
            send_sem=mode_send.at[k * gzs + turn],
            recv_sem=mode_recv.at[k * gzs + turn],
            device_id=(me, target), device_id_type=MESH,
        )

    def send_modes(k):

        def one(turn, carry):
            mode_copy(k, turn, ring).start()
            return carry

        lax.fori_loop(1, gzs, one, 0)

    for k in range(LIVE_DEV):

        def early(part_at, carry):
            forward(1, 2 * k + part_at)
            planes(k, part_at)
            return carry

        lax.fori_loop(0, 2, early, 0)
        send_modes(k)
    forward(1, jnp.int32(PIECES))

    def pair_modes(k, pair):
        stacked = []
        for q in (2 * pair, 2 * pair + 1):
            mine = modes[k][:, q, :]
            turned = pltpu.roll(mine, 64, 1) * sign_of
            stacked.append(jnp.concatenate([mine, turned], axis=0))
        third = dot((tz[0], tz[1]), split(jnp.concatenate(stacked, axis=1)))
        for n in range(2):
            value = third[:, 128 * n : 128 * n + 128]
            add_bins(k, 2 * pair + n, value * value * weight)

    for k in range(LIVE_DEV):

        def arrive(turn, carry):
            mode_copy(k, turn, (ring + gzs - turn) % gzs).wait_recv()
            mode_copy(k, turn, ring).wait_send()
            return carry

        def middle(part_at, carry):
            forward(2, 2 * k + part_at)

            def go(pair, c):
                pair_modes(k, part_at * (per // 4) + pair)
                return c

            lax.fori_loop(0, per // 4, go, 0)
            return carry

        lax.fori_loop(1, gzs, arrive, 0)
        modes[k][pl.ds(ring * depth, depth)] = sent[k][ring]
        lax.fori_loop(0, 2, middle, 0)
    forward(2, jnp.int32(PIECES))

    at_lane = lax.broadcasted_iota(jnp.int32, (NBINS, 128), 1)
    at_row = lax.broadcasted_iota(jnp.int32, (NBINS, 128), 0)
    rows = []
    for k in range(LIVE_DEV + 1):
        summed = jnp.sum(jnp.sum(acc[k], axis=1), axis=1, keepdims=True)
        rows.append(jnp.sum(jnp.where(at_lane == at_row, summed, 0.0), axis=0, keepdims=True))
    own_part[...] = jnp.concatenate(rows + [jnp.zeros((8 - LIVE_DEV - 1, 128), jnp.float32)], axis=0)

    def part_copy(turn, to):
        return pltpu.make_async_remote_copy(
            src_ref=own_part, dst_ref=part.at[to],
            send_sem=part_send.at[turn], recv_sem=part_recv.at[turn],
            device_id=(me, (ring + turn) % gzs), device_id_type=MESH,
        )

    def part_start(turn, carry):
        part_copy(turn, ring).start()
        return carry

    def part_wait(turn, carry):
        part_copy(turn, (ring + gzs - turn) % gzs).wait_recv()
        part_copy(turn, ring).wait_send()
        return carry

    lax.fori_loop(1, gzs, part_start, 0)

    total = jnp.int32(0)
    slots = [jnp.int32(0)] * rep_dev

    def position_of(p, found):
        slot = dest[p]
        return tuple(jnp.where(slot == me * rep_dev + j, p, found[j]) for j in range(rep_dev))

    found = lax.fori_loop(0, reps * rep_dev, position_of, tuple(slots))

    def look(i, state):
        total, rank, owners, ranks = state
        number = counts[i]
        rank = jnp.where(i % rep_dev == 0, 0, rank)
        ends = total + number
        hits = [(found[j] >= total) & (found[j] < ends) for j in range(rep_dev)]
        owners = tuple(jnp.where(hits[j], i // rep_dev, owners[j]) for j in range(rep_dev))
        ranks = tuple(jnp.where(hits[j], rank, ranks[j]) for j in range(rep_dev))
        return ends, rank + (number > 0).astype(jnp.int32), owners, ranks

    _, _, owners, ranks = lax.fori_loop(
        0, reps * rep_dev, look, (total, jnp.int32(0), tuple(slots), tuple(slots))
    )

    lax.fori_loop(1, gzs, part_wait, 0)
    part[ring] = own_part[...]
    binned = jnp.sum(part[...], axis=0)
    whole = binned[LIVE_DEV : LIVE_DEV + 1]
    used = lax.broadcasted_iota(jnp.int32, (8, 128), 1) < NBINS
    own_prop[...] = jnp.where(used, binned / jnp.where(used, float(L**3) * whole, 1.0), 0.0)

    def prop_copy(turn, to):
        return pltpu.make_async_remote_copy(
            src_ref=own_prop, dst_ref=props.at[to],
            send_sem=prop_send.at[turn], recv_sem=prop_recv.at[turn],
            device_id=((me + turn) % reps, ring), device_id_type=MESH,
        )

    def prop_start(turn, carry):
        prop_copy(turn, me).start()
        return carry

    def prop_wait(turn, carry):
        prop_copy(turn, (me + reps - turn) % reps).wait_recv()
        prop_copy(turn, me).wait_send()
        return carry

    lax.fori_loop(1, reps, prop_start, 0)

    def late(step, carry):
        forward(3 + step // (PIECES + 1), step % (PIECES + 1))
        return carry

    lax.fori_loop(0, (levels - 3) * (PIECES + 1), late, 0)

    lax.fori_loop(1, reps, prop_wait, 0)
    props[me] = own_prop[...]
    for j in range(rep_dev):
        prop[j : j + 1, :] = props[owners[j], pl.ds(ranks[j], 1), :][:, :NBINS]

    def from_mate(step, carry):
        origin, index = step // PIECES, step % PIECES

        @pl.when(index > 0)
        def _():
            send(origin * COLUMNS + 1 - x, index, own_x_sem.at[index], mate).wait_recv()

        return carry

    lax.fori_loop(0, levels * PIECES, from_mate, 0)

    half = CHUNKS * 64
    for j in range(rep_dev):
        for h in range(2):
            out[j, :, half * h : half * h + half] = gathered[owners[j] * LIVE_DEV + ranks[j], h]

    def drain(index, carry):
        send(me, index, own_x_sem.at[index], mate).wait_send()
        for origin, x_sem, last in ((0, up_x_sem, levels - 1), (levels - 1, down_x_sem, 0)):

            @pl.when((z == last) & (index > 0))
            def _():
                send(origin * COLUMNS + x, index, x_sem.at[index], mate).wait_send()

        return carry

    lax.fori_loop(0, PIECES, drain, 0)


def local(lattice_field, langevin_noise, masses, counts, dest_slots, mode_bins):
    rep_dev, depth, sites = lattice_field.shape
    reps, gzs = lax.axis_size("rep"), lax.axis_size("gz")
    per = L // gzs
    levels = reps // COLUMNS
    assert levels >= 4
    f32, dma = jnp.float32, pltpu.SemaphoreType.DMA
    scratch = [
        pltpu.VMEM((SWEEPS * LIVE_DEV, depth + 16, sites), f32),
        pltpu.VMEM((reps * LIVE_DEV, 2, depth, sites // 2), f32),
        pltpu.VMEM((SWEEPS, 2, LIVE_DEV, 1, sites), f32),
        pltpu.VMEM((SWEEPS, 2, LIVE_DEV, 1, sites), f32),
        pltpu.VMEM((LIVE_DEV, depth * CHUNKS, 128), f32),
        *[pltpu.VMEM((gzs, depth, per, 128), f32)] * LIVE_DEV,
        *[pltpu.VMEM((L, per, 128), f32)] * LIVE_DEV,
        pltpu.VMEM((per, L, 128), jnp.int32),
        pltpu.VMEM((LIVE_DEV + 1, NBINS, 8, 128), f32),
        pltpu.VMEM((gzs, 8, 128), f32),
        pltpu.VMEM((reps, 8, 128), f32),
        pltpu.VMEM((8, 128), f32),
        pltpu.VMEM((8, 128), f32),
        dma((PIECES + 1,)),
        dma((PIECES + 1,)),
        dma((PIECES,)),
        dma((PIECES,)),
        dma((PIECES,)),
        dma((reps * PIECES,)),
        dma((SWEEPS, 2, LIVE_DEV)),
        dma((SWEEPS, 2, LIVE_DEV)),
        dma((LIVE_DEV * gzs,)),
        dma((LIVE_DEV * gzs,)),
        dma((gzs,)),
        dma((gzs,)),
        dma((reps,)),
        dma((reps,)),
    ]
    smem = pl.BlockSpec(memory_space=pltpu.SMEM)
    vmem = pl.BlockSpec(memory_space=pltpu.VMEM)
    return pl.pallas_call(
        functools.partial(kernel, reps, gzs, rep_dev),
        out_shape=(
            jax.ShapeDtypeStruct(lattice_field.shape, f32),
            jax.ShapeDtypeStruct((rep_dev, NBINS), f32),
        ),
        in_specs=[smem, smem] + [vmem] * 7,
        out_specs=(vmem, vmem),
        scratch_shapes=scratch,
        compiler_params=pltpu.CompilerParams(
            collective_id=0, has_side_effects=True, vmem_limit_bytes=56 * 1024 * 1024
        ),
    )(counts, dest_slots, lattice_field, langevin_noise, masses, mode_bins, *map(jnp.asarray, tables()))


def solution(mesh):
    in_specs = (
        P("rep", "gz", None),
        P(None, "rep", "gz", None),
        P("gz", None),
        P(),
        P(),
        P("gz", None, None),
    )
    out_specs = (P("rep", "gz", None), P("rep", None))
    return jax.shard_map(local, mesh=mesh, in_specs=in_specs, out_specs=out_specs, check_vma=False)
```

```python
import functools

import jax
import jax.numpy as jnp
import numpy as np
from jax import lax
from jax.experimental import pallas as pl
from jax.experimental.pallas import tpu as pltpu
from jax.sharding import PartitionSpec as P

L = 64
HALF = L // 2 + 1
SWEEPS = 2
NBINS = 16
LIVE_DEV = 3
COLUMNS = 2
PIECES = 2 * LIVE_DEV
CHUNKS = L * L // 128

step_size = 0.1
quartic = 0.5
kick = float(np.sqrt(np.float32(2.0 * step_size)))
MESH = pl.DeviceIdType.MESH


def tables():
    angle = 2.0 * np.pi / L * (np.outer(np.arange(L), np.arange(L)) % L)
    cos, sin = np.cos(angle), np.sin(angle)
    along_x = np.zeros((128, 512))
    for parity in range(2):
        rows = slice(64 * parity, 64 * parity + 64)
        at = 128 * parity
        along_x[rows, at : at + HALF] = cos[:, :HALF]
        along_x[rows, at + 64 : at + 64 + HALF] = -sin[:, :HALF]
        at = 256 + 128 * parity
        along_x[rows, at : at + HALF] = -sin[:, :HALF]
        along_x[rows, at + 64 : at + 64 + HALF] = -cos[:, :HALF]
    along_y = np.concatenate([cos[:, 0::2], cos[:, 1::2], sin[:, 0::2], sin[:, 1::2]], axis=1)
    along_z = np.concatenate([cos, sin], axis=1)

    def halves(table):
        table = table.astype(np.float32)
        high = table.astype(jnp.bfloat16)
        return np.stack([high, (table - high.astype(np.float32)).astype(jnp.bfloat16)])

    return halves(along_x), halves(along_y), halves(along_z)


def split(value):
    high = value.astype(jnp.bfloat16)
    return high, (value - high.astype(jnp.float32)).astype(jnp.bfloat16)


def dot(left, right):
    def one(a, b):
        return jnp.dot(a, b, preferred_element_type=jnp.float32)

    return one(left[0], right[0]) + (one(left[0], right[1]) + one(left[1], right[0]))


def kernel(reps, gzs, rep_dev, counts, dest, field, noise_in, masses, bins_in, tx, ty, tz, gathered, chosen, prop, *scratch):
    (
        swept, noise0, noise1, own0, own1, own2, edge_out, edge_in, work, sent0, sent1, sent2, modes0, modes1, modes2, bins, acc, part, props, own_part, own_prop,
        up_sem, down_sem, own_x_sem, up_x_sem, down_x_sem, recv_sem,
        edge_send, edge_recv, mode_send, mode_recv, part_send, part_recv, prop_send, prop_recv, noise_sem, keep_sem,
    ) = scratch
    own, noise = (own0, own1, own2), (noise0, noise1)
    sent, modes = (sent0, sent1, sent2), (modes0, modes1, modes2)
    depth = field.shape[1]
    per = L // gzs
    levels = reps // COLUMNS
    me, ring = lax.axis_index("rep"), lax.axis_index("gz")
    z, x = me // COLUMNS, me % COLUMNS
    mate = z * COLUMNS + (1 - x)

    barrier = pltpu.get_barrier_semaphore()

    def greet(turn, carry):
        pl.semaphore_signal(barrier, inc=1, device_id=(me, (ring + turn) % gzs), device_id_type=MESH)
        return carry

    def greet_rep(turn, carry):
        pl.semaphore_signal(barrier, inc=1, device_id=((me + turn) % reps, ring), device_id_type=MESH)
        return carry

    lax.fori_loop(1, gzs, greet, 0)
    lax.fori_loop(1, reps, greet_rep, 0)

    def noise_copy(turn):
        return pltpu.make_async_copy(noise_in.at[turn], noise[turn], noise_sem.at[turn])

    for turn in range(SWEEPS):
        noise_copy(turn).start()

    live = [jnp.int32(0)] * LIVE_DEV
    rank = jnp.int32(0)
    for i in range(rep_dev):
        alive = counts[me * rep_dev + i] > 0
        live = [jnp.where(alive & (rank == k), i, live[k]) for k in range(LIVE_DEV)]
        rank = rank + alive.astype(jnp.int32)

    lane = lax.broadcasted_iota(jnp.int32, (depth, 128), 1)
    first_x, last_x, even_y = lane % 64 == 0, lane % 64 == 63, lane < 64

    def send_own(index, sem, target):
        return pltpu.make_async_remote_copy(
            src_ref=own[index // 2].at[index % 2], dst_ref=piece(me, index), send_sem=sem,
            recv_sem=recv_sem.at[me * PIECES + index], device_id=(target, ring), device_id_type=MESH,
        )

    def edge_copy(turn, side, k):
        target = (ring + 1) % gzs if side == 0 else (ring + gzs - 1) % gzs
        return pltpu.make_async_remote_copy(
            src_ref=edge_out.at[turn, side, k], dst_ref=edge_in.at[turn, side, k],
            send_sem=edge_send.at[turn, side, k], recv_sem=edge_recv.at[turn, side, k],
            device_id=(me, target), device_id_type=MESH,
        )

    def edge_rows(turn, k):
        edge_out[turn, 0, k] = swept[turn * LIVE_DEV + k, 8 + depth - 1 : 8 + depth, :]
        edge_out[turn, 1, k] = swept[turn * LIVE_DEV + k, 8:9, :]

    def edge_start(turn, k):
        for side in range(2):
            edge_copy(turn, side, k).start()

    def edge_wait(turn, k):
        for side in range(2):
            edge_copy(turn, side, k).wait()
        swept[turn * LIVE_DEV + k, 7:8, :] = edge_in[turn, 0, k]
        swept[turn * LIVE_DEV + k, 8 + depth : 9 + depth, :] = edge_in[turn, 1, k]

    def piece(owner, index):
        return gathered.at[owner * LIVE_DEV + index // 2, index % 2]

    def send(owner, index, sem, target):
        ref = piece(owner, index)
        return pltpu.make_async_remote_copy(
            src_ref=ref, dst_ref=ref, send_sem=sem, recv_sem=recv_sem.at[owner * PIECES + index],
            device_id=(target, ring), device_id_type=MESH,
        )

    for k in range(LIVE_DEV):
        swept[k, 8 : 8 + depth, :] = field[live[k]]
        edge_rows(0, k)
    pl.semaphore_wait(barrier, gzs - 1 + reps - 1)
    for k in range(LIVE_DEV):
        edge_start(0, k)

    narrow = lax.broadcasted_iota(jnp.int32, (per, 128), 1) % 64 < HALF
    for kz in range(HALF):
        mine = bins_in[kz]
        mine = jnp.where(narrow, jnp.concatenate([mine, mine], axis=1), -1)
        bins[:, kz, :] = mine
        if 0 < kz < L // 2:
            bins[:, L - kz, :] = mine
    acc[...] = jnp.zeros(acc.shape, jnp.float32)
    wide = lax.broadcasted_iota(jnp.int32, (L, 128), 1)
    wave_x = wide % 64
    weight = jnp.where((wave_x == 0) | (wave_x == L // 2), 1.0, 2.0).astype(jnp.float32)
    sign_of = jnp.where(wide < 64, 1.0, -1.0).astype(jnp.float32)
    real_weight = jnp.where(wide < 64, weight, 0.0)

    def add_bins(k, q, value):
        here = bins[q]
        for b in range(NBINS):
            taken = jnp.where(here == b, value, 0.0)
            acc[k, b] += jnp.sum(taken.reshape(L // 8, 8, 128), axis=0)

    def weigh(q, carry):
        add_bins(LIVE_DEV, q, real_weight)
        return carry

    lax.fori_loop(0, per, weigh, 0)

    def keep(k):
        return pltpu.make_async_copy(own[k], gathered.at[me * LIVE_DEV + k], keep_sem.at[k])

    def sweep(turn, k):
        edge_wait(turn, k)
        from_at, to_at = turn * LIVE_DEV + k, (turn + 1) * LIVE_DEV + k

        def block(j, carry):
            def lanes(at):
                return pl.ds(pl.multiple_of(at % CHUNKS * 128, 128), 128)

            here = lanes(j)
            center = swept[from_at, 8 : 8 + depth, here]
            before = pltpu.roll(swept[from_at, 8 : 8 + depth, lanes(j + CHUNKS - 1)], 64, 1)
            after = pltpu.roll(swept[from_at, 8 : 8 + depth, lanes(j + 1)], 64, 1)
            beside = swept[from_at, 7 : 7 + depth, here] + swept[from_at, 9 : 9 + depth, here]
            beside += pltpu.roll(center, 64, 1) + jnp.where(even_y, before, after)
            beside += jnp.where(first_x, pltpu.roll(center, 65, 1), pltpu.roll(center, 1, 1))
            beside += jnp.where(last_x, pltpu.roll(center, 63, 1), pltpu.roll(center, 127, 1))
            drift = 6.0 * center - beside + masses[:, here] * center + quartic * center * center * center
            fresh = center - step_size * drift + kick * noise[turn][live[k], :, here]
            if turn + 1 < SWEEPS:
                swept[to_at, 8 : 8 + depth, here] = fresh
            else:
                at = pl.ds(pl.multiple_of(j % (CHUNKS // 2) * 128, 128), 128)
                own[k][j // (CHUNKS // 2), :, at] = fresh
                work[k, pl.ds(j, depth, stride=CHUNKS), :] = fresh
            return carry

        if turn + 1 < SWEEPS:
            lax.fori_loop(0, CHUNKS, block, 0, unroll=8)
            edge_rows(turn + 1, k)
            edge_start(turn + 1, k)
            return
        for h in range(2):
            lax.fori_loop(h * CHUNKS // 2, (h + 1) * CHUNKS // 2, block, 0, unroll=8)
            index = 2 * k + h
            send_own(index, own_x_sem.at[index], mate).start()

            @pl.when(z + 1 < levels)
            def _():
                send_own(index, up_sem.at[index], me + COLUMNS).start()

            @pl.when(z > 0)
            def _():
                send_own(index, down_sem.at[index], me - COLUMNS).start()

        keep(k).start()

    noise_copy(0).wait()
    sweep(0, 0)
    noise_copy(1).wait()
    for k in range(1, LIVE_DEV):
        sweep(0, k)
        sweep(1, k - 1)
    sweep(1, LIVE_DEV - 1)

    send(mate, 0, own_x_sem.at[0], mate).wait_recv()

    @pl.when(z + 1 < levels)
    def _():
        send(mate, 0, up_sem.at[PIECES], me + COLUMNS).start()

    @pl.when(z > 0)
    def _():
        send(mate, 0, down_sem.at[PIECES], me - COLUMNS).start()

    def forward(t, at):
        foreign = (at == PIECES).astype(jnp.int32)
        index = at - PIECES * foreign
        column = x + foreign * (1 - 2 * x)
        for sign, sem, x_sem, edge in ((1, up_sem, up_x_sem, levels - 1), (-1, down_sem, down_x_sem, 0)):
            origin = z - sign * t
            owner = origin * COLUMNS + column
            before = (origin + sign) * COLUMNS + column

            @pl.when((origin >= 0) & (origin < levels))
            def _():
                send(owner, index, sem.at[at], mate).wait_recv()

            @pl.when((origin + sign >= 0) & (origin + sign < levels) & (z != edge))
            def _():
                send(before, index, sem.at[at], me + sign * COLUMNS).wait_send()

            @pl.when((origin >= 0) & (origin < levels) & (z != edge))
            def _():
                send(owner, index, sem.at[at], me + sign * COLUMNS).start()

            @pl.when((t > 1) & (origin + sign >= 0) & (origin + sign < levels) & (at < PIECES) & (at > 0))
            def _():
                send(before, index, x_sem.at[index], mate).wait_send()

            @pl.when((origin >= 0) & (origin < levels) & (at < PIECES) & (at > 0))
            def _():
                send(owner, index, x_sem.at[index], mate).start()

    half_depth = depth // 2

    def planes(k, part_at):
        rows = half_depth * CHUNKS
        value = work[k, pl.ds(pl.multiple_of(part_at * rows, rows), rows), :]
        first = dot(split(value), (tx[0], tx[1]))
        for pair in range(half_depth // 2):
            stacked = []
            for plane in (2 * pair, 2 * pair + 1):
                mine = first[plane * CHUNKS : (plane + 1) * CHUNKS]
                stacked.append(jnp.concatenate([mine[:, 128 * c : 128 * c + 128] for c in range(4)], axis=0))
            second = dot((ty[0], ty[1]), split(jnp.concatenate(stacked, axis=1)))
            for d in range(gzs):
                rows = second[d * per : (d + 1) * per]
                at = part_at * half_depth + 2 * pair
                sent[k][d, at] = rows[:, :128]
                sent[k][d, at + 1] = rows[:, 128:]

    def mode_copy(k, turn, source):
        target = (ring + turn) % gzs
        return pltpu.make_async_remote_copy(
            src_ref=sent[k].at[target],
            dst_ref=modes[k].at[pl.ds(source * depth, depth)],
            send_sem=mode_send.at[k * gzs + turn],
            recv_sem=mode_recv.at[k * gzs + turn],
            device_id=(me, target), device_id_type=MESH,
        )

    def send_modes(k):

        def one(turn, carry):
            mode_copy(k, turn, ring).start()
            return carry

        lax.fori_loop(1, gzs, one, 0)

    for k in range(LIVE_DEV):

        def early(part_at, carry):
            forward(1, 2 * k + part_at)
            planes(k, part_at)
            return carry

        lax.fori_loop(0, 2, early, 0)
        send_modes(k)
    forward(1, jnp.int32(PIECES))

    def pair_modes(k, pair):
        stacked = []
        for q in (2 * pair, 2 * pair + 1):
            mine = modes[k][:, q, :]
            turned = pltpu.roll(mine, 64, 1) * sign_of
            stacked.append(jnp.concatenate([mine, turned], axis=0))
        third = dot((tz[0], tz[1]), split(jnp.concatenate(stacked, axis=1)))
        for n in range(2):
            value = third[:, 128 * n : 128 * n + 128]
            add_bins(k, 2 * pair + n, value * value * weight)

    for k in range(LIVE_DEV):

        def arrive(turn, carry):
            mode_copy(k, turn, (ring + gzs - turn) % gzs).wait_recv()
            mode_copy(k, turn, ring).wait_send()
            return carry

        def middle(part_at, carry):
            forward(2, 2 * k + part_at)

            def go(pair, c):
                pair_modes(k, part_at * (per // 4) + pair)
                return c

            lax.fori_loop(0, per // 4, go, 0)
            return carry

        lax.fori_loop(1, gzs, arrive, 0)
        modes[k][pl.ds(ring * depth, depth)] = sent[k][ring]
        lax.fori_loop(0, 2, middle, 0)
    forward(2, jnp.int32(PIECES))

    at_lane = lax.broadcasted_iota(jnp.int32, (NBINS, 128), 1)
    at_row = lax.broadcasted_iota(jnp.int32, (NBINS, 128), 0)
    rows = []
    for k in range(LIVE_DEV + 1):
        summed = jnp.sum(jnp.sum(acc[k], axis=1), axis=1, keepdims=True)
        rows.append(jnp.sum(jnp.where(at_lane == at_row, summed, 0.0), axis=0, keepdims=True))
    own_part[...] = jnp.concatenate(rows + [jnp.zeros((8 - LIVE_DEV - 1, 128), jnp.float32)], axis=0)

    def part_copy(turn, to):
        return pltpu.make_async_remote_copy(
            src_ref=own_part, dst_ref=part.at[to],
            send_sem=part_send.at[turn], recv_sem=part_recv.at[turn],
            device_id=(me, (ring + turn) % gzs), device_id_type=MESH,
        )

    def part_start(turn, carry):
        part_copy(turn, ring).start()
        return carry

    def part_wait(turn, carry):
        part_copy(turn, (ring + gzs - turn) % gzs).wait_recv()
        part_copy(turn, ring).wait_send()
        return carry

    lax.fori_loop(1, gzs, part_start, 0)

    total = jnp.int32(0)
    slots = [jnp.int32(0)] * rep_dev

    def position_of(p, found):
        slot = dest[p]
        return tuple(jnp.where(slot == me * rep_dev + j, p, found[j]) for j in range(rep_dev))

    found = lax.fori_loop(0, reps * rep_dev, position_of, tuple(slots))

    def look(i, state):
        total, rank, owners, ranks = state
        number = counts[i]
        rank = jnp.where(i % rep_dev == 0, 0, rank)
        ends = total + number
        hits = [(found[j] >= total) & (found[j] < ends) for j in range(rep_dev)]
        owners = tuple(jnp.where(hits[j], i // rep_dev, owners[j]) for j in range(rep_dev))
        ranks = tuple(jnp.where(hits[j], rank, ranks[j]) for j in range(rep_dev))
        return ends, rank + (number > 0).astype(jnp.int32), owners, ranks

    _, _, owners, ranks = lax.fori_loop(
        0, reps * rep_dev, look, (total, jnp.int32(0), tuple(slots), tuple(slots))
    )

    lax.fori_loop(1, gzs, part_wait, 0)
    part[ring] = own_part[...]
    binned = jnp.sum(part[...], axis=0)
    whole = binned[LIVE_DEV : LIVE_DEV + 1]
    used = lax.broadcasted_iota(jnp.int32, (8, 128), 1) < NBINS
    own_prop[...] = jnp.where(used, binned / jnp.where(used, float(L**3) * whole, 1.0), 0.0)

    def prop_copy(turn, to):
        return pltpu.make_async_remote_copy(
            src_ref=own_prop, dst_ref=props.at[to],
            send_sem=prop_send.at[turn], recv_sem=prop_recv.at[turn],
            device_id=((me + turn) % reps, ring), device_id_type=MESH,
        )

    def prop_start(turn, carry):
        prop_copy(turn, me).start()
        return carry

    def prop_wait(turn, carry):
        prop_copy(turn, (me + reps - turn) % reps).wait_recv()
        prop_copy(turn, me).wait_send()
        return carry

    lax.fori_loop(1, reps, prop_start, 0)

    def late(step, carry):
        forward(3 + step // (PIECES + 1), step % (PIECES + 1))
        return carry

    lax.fori_loop(0, (levels - 3) * (PIECES + 1), late, 0)

    lax.fori_loop(1, reps, prop_wait, 0)
    props[me] = own_prop[...]
    for j in range(rep_dev):
        prop[j : j + 1, :] = props[owners[j], pl.ds(ranks[j], 1), :][:, :NBINS]

    for k in range(LIVE_DEV):
        keep(k).wait()

    def from_mate(step, carry):
        origin, index = step // PIECES, step % PIECES

        @pl.when(index > 0)
        def _():
            send(origin * COLUMNS + 1 - x, index, own_x_sem.at[index], mate).wait_recv()

        return carry

    lax.fori_loop(0, levels * PIECES, from_mate, 0)

    for j in range(rep_dev):
        chosen[j] = owners[j] * LIVE_DEV + ranks[j]

    def drain(index, carry):
        send(me, index, own_x_sem.at[index], mate).wait_send()
        for origin, x_sem, last in ((0, up_x_sem, levels - 1), (levels - 1, down_x_sem, 0)):

            @pl.when((z == last) & (index > 0))
            def _():
                send(origin * COLUMNS + x, index, x_sem.at[index], mate).wait_send()

        return carry

    lax.fori_loop(0, PIECES, drain, 0)


def local(lattice_field, langevin_noise, masses, counts, dest_slots, mode_bins):
    rep_dev, depth, sites = lattice_field.shape
    reps, gzs = lax.axis_size("rep"), lax.axis_size("gz")
    per = L // gzs
    levels = reps // COLUMNS
    assert levels >= 4
    f32, dma = jnp.float32, pltpu.SemaphoreType.DMA
    scratch = [
        pltpu.VMEM((SWEEPS * LIVE_DEV, depth + 16, sites), f32),
        *[pltpu.VMEM((rep_dev, depth, sites), f32)] * SWEEPS,
        *[pltpu.VMEM((2, depth, sites // 2), f32)] * LIVE_DEV,
        pltpu.VMEM((SWEEPS, 2, LIVE_DEV, 1, sites), f32),
        pltpu.VMEM((SWEEPS, 2, LIVE_DEV, 1, sites), f32),
        pltpu.VMEM((LIVE_DEV, depth * CHUNKS, 128), f32),
        *[pltpu.VMEM((gzs, depth, per, 128), f32)] * LIVE_DEV,
        *[pltpu.VMEM((L, per, 128), f32)] * LIVE_DEV,
        pltpu.VMEM((per, L, 128), jnp.int32),
        pltpu.VMEM((LIVE_DEV + 1, NBINS, 8, 128), f32),
        pltpu.VMEM((gzs, 8, 128), f32),
        pltpu.VMEM((reps, 8, 128), f32),
        pltpu.VMEM((8, 128), f32),
        pltpu.VMEM((8, 128), f32),
        dma((PIECES + 1,)),
        dma((PIECES + 1,)),
        dma((PIECES,)),
        dma((PIECES,)),
        dma((PIECES,)),
        dma((reps * PIECES,)),
        dma((SWEEPS, 2, LIVE_DEV)),
        dma((SWEEPS, 2, LIVE_DEV)),
        dma((LIVE_DEV * gzs,)),
        dma((LIVE_DEV * gzs,)),
        dma((gzs,)),
        dma((gzs,)),
        dma((reps,)),
        dma((reps,)),
        dma((SWEEPS,)),
        dma((LIVE_DEV,)),
    ]
    smem = pl.BlockSpec(memory_space=pltpu.SMEM)
    vmem = pl.BlockSpec(memory_space=pltpu.VMEM)
    hbm = pl.BlockSpec(memory_space=pl.ANY)
    gathered, chosen, propagator = pl.pallas_call(
        functools.partial(kernel, reps, gzs, rep_dev),
        out_shape=(
            jax.ShapeDtypeStruct((reps * LIVE_DEV, 2, depth, sites // 2), f32),
            jax.ShapeDtypeStruct((rep_dev,), jnp.int32),
            jax.ShapeDtypeStruct((rep_dev, NBINS), f32),
        ),
        in_specs=[smem, smem, vmem, hbm, vmem, vmem, vmem, vmem, vmem],
        out_specs=(hbm, smem, vmem),
        scratch_shapes=scratch,
        compiler_params=pltpu.CompilerParams(
            collective_id=0, has_side_effects=True, vmem_limit_bytes=56 * 1024 * 1024
        ),
    )(
        counts, dest_slots, lattice_field, langevin_noise, masses,
        jnp.transpose(mode_bins, (2, 0, 1)), *map(jnp.asarray, tables()),
    )
    return pl.pallas_call(
        pick,
        out_shape=(
            jax.ShapeDtypeStruct(lattice_field.shape, f32),
            jax.ShapeDtypeStruct((rep_dev, NBINS), f32),
        ),
        grid_spec=pltpu.PrefetchScalarGridSpec(
            num_scalar_prefetch=1,
            grid=(rep_dev,),
            in_specs=[
                pl.BlockSpec((1, 2, depth, sites // 2), lambda j, chosen: (chosen[j], 0, 0, 0)),
                pl.BlockSpec((rep_dev, NBINS), lambda j, chosen: (0, 0)),
            ],
            out_specs=(
                pl.BlockSpec((1, depth, sites), lambda j, chosen: (j, 0, 0)),
                pl.BlockSpec((rep_dev, NBINS), lambda j, chosen: (0, 0)),
            ),
        ),
        compiler_params=pltpu.CompilerParams(vmem_limit_bytes=16 * 1024 * 1024),
    )(chosen, gathered, propagator)


def pick(chosen, slab, prop, out, prop_out):
    half = slab.shape[3]
    out[0, :, :half] = slab[0, 0]
    out[0, :, half:] = slab[0, 1]
    prop_out[...] = prop[...]


def solution(mesh):
    in_specs = (
        P("rep", "gz", None),
        P(None, "rep", "gz", None),
        P("gz", None),
        P(),
        P(),
        P("gz", None, None),
    )
    out_specs = (P("rep", "gz", None), P("rep", None))
    return jax.shard_map(local, mesh=mesh, in_specs=in_specs, out_specs=out_specs, check_vma=False)
```

```python
import functools

import jax
import jax.numpy as jnp
import numpy as np
from jax import lax
from jax.experimental import pallas as pl
from jax.experimental.pallas import tpu as pltpu
from jax.sharding import PartitionSpec as P

L = 64
HALF = L // 2 + 1
SWEEPS = 2
NBINS = 16
LIVE_DEV = 3
COLUMNS = 2
PIECES = 2 * LIVE_DEV
CHUNKS = L * L // 128

step_size = 0.1
quartic = 0.5
kick = float(np.sqrt(np.float32(2.0 * step_size)))
MESH = pl.DeviceIdType.MESH


def tables():
    angle = 2.0 * np.pi / L * (np.outer(np.arange(L), np.arange(L)) % L)
    cos, sin = np.cos(angle), np.sin(angle)
    along_x = np.zeros((128, 512))
    for parity in range(2):
        rows = slice(64 * parity, 64 * parity + 64)
        at = 128 * parity
        along_x[rows, at : at + HALF] = cos[:, :HALF]
        along_x[rows, at + 64 : at + 64 + HALF] = -sin[:, :HALF]
        at = 256 + 128 * parity
        along_x[rows, at : at + HALF] = -sin[:, :HALF]
        along_x[rows, at + 64 : at + 64 + HALF] = -cos[:, :HALF]
    along_y = np.concatenate([cos[:, 0::2], cos[:, 1::2], sin[:, 0::2], sin[:, 1::2]], axis=1)
    along_z = np.concatenate([cos, sin], axis=1)

    def halves(table):
        table = table.astype(np.float32)
        high = table.astype(jnp.bfloat16)
        return np.stack([high, (table - high.astype(np.float32)).astype(jnp.bfloat16)])

    return halves(along_x), halves(along_y), halves(along_z)


def split(value):
    high = value.astype(jnp.bfloat16)
    return high, (value - high.astype(jnp.float32)).astype(jnp.bfloat16)


def dot(left, right):
    def one(a, b):
        return jnp.dot(a, b, preferred_element_type=jnp.float32)

    return one(left[0], right[0]) + (one(left[0], right[1]) + one(left[1], right[0]))


def kernel(reps, gzs, rep_dev, counts, dest, field, noise_in, masses, bins_in, tx, ty, tz, gathered, chosen, prop, *scratch):
    (
        swept, noise0, noise1, own0, own1, own2, edge_out, edge_in, work, sent0, sent1, sent2, modes0, modes1, modes2, bins, acc, part, props, own_part, own_prop,
        up_sem, down_sem, own_x_sem, up_x_sem, down_x_sem, recv_sem,
        edge_send, edge_recv, mode_send, mode_recv, part_send, part_recv, prop_send, prop_recv, noise_sem, keep_sem,
    ) = scratch
    own, noise = (own0, own1, own2), (noise0, noise1)
    sent, modes = (sent0, sent1, sent2), (modes0, modes1, modes2)
    depth = field.shape[1]
    per = L // gzs
    levels = reps // COLUMNS
    me, ring = lax.axis_index("rep"), lax.axis_index("gz")
    z, x = me // COLUMNS, me % COLUMNS
    mate = z * COLUMNS + (1 - x)

    barrier = pltpu.get_barrier_semaphore()

    def greet(turn, carry):
        pl.semaphore_signal(barrier, inc=1, device_id=(me, (ring + turn) % gzs), device_id_type=MESH)
        return carry

    def greet_rep(turn, carry):
        pl.semaphore_signal(barrier, inc=1, device_id=((me + turn) % reps, ring), device_id_type=MESH)
        return carry

    lax.fori_loop(1, gzs, greet, 0)
    lax.fori_loop(1, reps, greet_rep, 0)

    def noise_copy(turn):
        return pltpu.make_async_copy(noise_in.at[turn], noise[turn], noise_sem.at[turn])

    for turn in range(SWEEPS):
        noise_copy(turn).start()

    live = [jnp.int32(0)] * LIVE_DEV
    rank = jnp.int32(0)
    for i in range(rep_dev):
        alive = counts[me * rep_dev + i] > 0
        live = [jnp.where(alive & (rank == k), i, live[k]) for k in range(LIVE_DEV)]
        rank = rank + alive.astype(jnp.int32)

    lane = lax.broadcasted_iota(jnp.int32, (depth, 128), 1)
    first_x, last_x, even_y = lane % 64 == 0, lane % 64 == 63, lane < 64

    def send_own(index, sem, target):
        return pltpu.make_async_remote_copy(
            src_ref=own[index // 2].at[index % 2], dst_ref=piece(me, index), send_sem=sem,
            recv_sem=recv_sem.at[me * PIECES + index], device_id=(target, ring), device_id_type=MESH,
        )

    def edge_copy(turn, side, k):
        target = (ring + 1) % gzs if side == 0 else (ring + gzs - 1) % gzs
        return pltpu.make_async_remote_copy(
            src_ref=edge_out.at[turn, side, k], dst_ref=edge_in.at[turn, side, k],
            send_sem=edge_send.at[turn, side, k], recv_sem=edge_recv.at[turn, side, k],
            device_id=(me, target), device_id_type=MESH,
        )

    def edge_rows(turn, k):
        edge_out[turn, 0, k] = swept[turn * LIVE_DEV + k, 8 + depth - 1 : 8 + depth, :]
        edge_out[turn, 1, k] = swept[turn * LIVE_DEV + k, 8:9, :]

    def edge_start(turn, k):
        for side in range(2):
            edge_copy(turn, side, k).start()

    def edge_wait(turn, k):
        for side in range(2):
            edge_copy(turn, side, k).wait()
        swept[turn * LIVE_DEV + k, 7:8, :] = edge_in[turn, 0, k]
        swept[turn * LIVE_DEV + k, 8 + depth : 9 + depth, :] = edge_in[turn, 1, k]

    def piece(owner, index):
        return gathered.at[owner * LIVE_DEV + index // 2, index % 2]

    def send(owner, index, sem, target):
        ref = piece(owner, index)
        return pltpu.make_async_remote_copy(
            src_ref=ref, dst_ref=ref, send_sem=sem, recv_sem=recv_sem.at[owner * PIECES + index],
            device_id=(target, ring), device_id_type=MESH,
        )

    for k in range(LIVE_DEV):
        swept[k, 8 : 8 + depth, :] = field[live[k]]
        edge_rows(0, k)
    pl.semaphore_wait(barrier, gzs - 1 + reps - 1)
    for k in range(LIVE_DEV):
        edge_start(0, k)

    narrow = lax.broadcasted_iota(jnp.int32, (per, 128), 1) % 64 < HALF
    for kz in range(HALF):
        mine = bins_in[kz]
        mine = jnp.where(narrow, jnp.concatenate([mine, mine], axis=1), -1)
        bins[:, kz, :] = mine
        if 0 < kz < L // 2:
            bins[:, L - kz, :] = mine
    acc[...] = jnp.zeros(acc.shape, jnp.float32)
    wide = lax.broadcasted_iota(jnp.int32, (L, 128), 1)
    wave_x = wide % 64
    weight = jnp.where((wave_x == 0) | (wave_x == L // 2), 1.0, 2.0).astype(jnp.float32)
    sign_of = jnp.where(wide < 64, 1.0, -1.0).astype(jnp.float32)
    real_weight = jnp.where(wide < 64, weight, 0.0)

    def add_bins(k, q, value):
        here = bins[q]
        for b in range(NBINS):
            taken = jnp.where(here == b, value, 0.0)
            acc[k, b] += jnp.sum(taken.reshape(L // 8, 8, 128), axis=0)

    def weigh(q, carry):
        add_bins(LIVE_DEV, q, real_weight)
        return carry

    lax.fori_loop(0, per, weigh, 0)

    def keep(k):
        return pltpu.make_async_copy(own[k], gathered.at[me * LIVE_DEV + k], keep_sem.at[k])

    def sweep(turn, k):
        edge_wait(turn, k)
        from_at, to_at = turn * LIVE_DEV + k, (turn + 1) * LIVE_DEV + k

        def block(j, carry):
            def lanes(at):
                return pl.ds(pl.multiple_of(at % CHUNKS * 128, 128), 128)

            here = lanes(j)
            center = swept[from_at, 8 : 8 + depth, here]
            before = pltpu.roll(swept[from_at, 8 : 8 + depth, lanes(j + CHUNKS - 1)], 64, 1)
            after = pltpu.roll(swept[from_at, 8 : 8 + depth, lanes(j + 1)], 64, 1)
            beside = swept[from_at, 7 : 7 + depth, here] + swept[from_at, 9 : 9 + depth, here]
            beside += pltpu.roll(center, 64, 1) + jnp.where(even_y, before, after)
            beside += jnp.where(first_x, pltpu.roll(center, 65, 1), pltpu.roll(center, 1, 1))
            beside += jnp.where(last_x, pltpu.roll(center, 63, 1), pltpu.roll(center, 127, 1))
            drift = 6.0 * center - beside + masses[:, here] * center + quartic * center * center * center
            fresh = center - step_size * drift + kick * noise[turn][live[k], :, here]
            if turn + 1 < SWEEPS:
                swept[to_at, 8 : 8 + depth, here] = fresh
            else:
                at = pl.ds(pl.multiple_of(j % (CHUNKS // 2) * 128, 128), 128)
                own[k][j // (CHUNKS // 2), :, at] = fresh
                work[k, pl.ds(j, depth, stride=CHUNKS), :] = fresh
            return carry

        if turn + 1 < SWEEPS:
            lax.fori_loop(0, CHUNKS, block, 0, unroll=8)
            edge_rows(turn + 1, k)
            edge_start(turn + 1, k)
            return
        for h in range(2):
            lax.fori_loop(h * CHUNKS // 2, (h + 1) * CHUNKS // 2, block, 0, unroll=8)
            index = 2 * k + h
            send_own(index, own_x_sem.at[index], mate).start()

            @pl.when(z + 1 < levels)
            def _():
                send_own(index, up_sem.at[index], me + COLUMNS).start()

            @pl.when(z > 0)
            def _():
                send_own(index, down_sem.at[index], me - COLUMNS).start()

        keep(k).start()

    noise_copy(0).wait()
    sweep(0, 0)
    noise_copy(1).wait()
    for k in range(1, LIVE_DEV):
        sweep(0, k)
        sweep(1, k - 1)
    sweep(1, LIVE_DEV - 1)

    send(mate, 0, own_x_sem.at[0], mate).wait_recv()

    @pl.when(z + 1 < levels)
    def _():
        send(mate, 0, up_sem.at[PIECES], me + COLUMNS).start()

    @pl.when(z > 0)
    def _():
        send(mate, 0, down_sem.at[PIECES], me - COLUMNS).start()

    def forward(t, at):
        foreign = (at == PIECES).astype(jnp.int32)
        index = at - PIECES * foreign
        column = x + foreign * (1 - 2 * x)
        for sign, sem, x_sem, edge in ((1, up_sem, up_x_sem, levels - 1), (-1, down_sem, down_x_sem, 0)):
            origin = z - sign * t
            owner = origin * COLUMNS + column
            before = (origin + sign) * COLUMNS + column

            @pl.when((origin >= 0) & (origin < levels))
            def _():
                send(owner, index, sem.at[at], mate).wait_recv()

            @pl.when((origin + sign >= 0) & (origin + sign < levels) & (z != edge))
            def _():
                send(before, index, sem.at[at], me + sign * COLUMNS).wait_send()

            @pl.when((origin >= 0) & (origin < levels) & (z != edge))
            def _():
                send(owner, index, sem.at[at], me + sign * COLUMNS).start()

            @pl.when((t > 1) & (origin + sign >= 0) & (origin + sign < levels) & (at < PIECES) & (at > 0))
            def _():
                send(before, index, x_sem.at[index], mate).wait_send()

            @pl.when((origin >= 0) & (origin < levels) & (at < PIECES) & (at > 0))
            def _():
                send(owner, index, x_sem.at[index], mate).start()

    half_depth = depth // 2

    def planes(k, part_at):
        rows = half_depth * CHUNKS
        value = work[k, pl.ds(pl.multiple_of(part_at * rows, rows), rows), :]
        first = dot(split(value), (tx[0], tx[1]))
        for pair in range(half_depth // 2):
            stacked = []
            for plane in (2 * pair, 2 * pair + 1):
                mine = first[plane * CHUNKS : (plane + 1) * CHUNKS]
                stacked.append(jnp.concatenate([mine[:, 128 * c : 128 * c + 128] for c in range(4)], axis=0))
            second = dot((ty[0], ty[1]), split(jnp.concatenate(stacked, axis=1)))
            for d in range(gzs):
                rows = second[d * per : (d + 1) * per]
                at = part_at * half_depth + 2 * pair
                sent[k][d, at] = rows[:, :128]
                sent[k][d, at + 1] = rows[:, 128:]

    def mode_copy(k, turn, source):
        target = (ring + turn) % gzs
        return pltpu.make_async_remote_copy(
            src_ref=sent[k].at[target],
            dst_ref=modes[k].at[pl.ds(source * depth, depth)],
            send_sem=mode_send.at[k * gzs + turn],
            recv_sem=mode_recv.at[k * gzs + turn],
            device_id=(me, target), device_id_type=MESH,
        )

    def send_modes(k):

        def one(turn, carry):
            mode_copy(k, turn, ring).start()
            return carry

        lax.fori_loop(1, gzs, one, 0)

    for k in range(LIVE_DEV):

        def early(part_at, carry):
            forward(1, 2 * k + part_at)
            planes(k, part_at)
            return carry

        lax.fori_loop(0, 2, early, 0)
        send_modes(k)
    forward(1, jnp.int32(PIECES))

    def pair_modes(k, pair):
        stacked = []
        for q in (2 * pair, 2 * pair + 1):
            mine = modes[k][:, q, :]
            turned = pltpu.roll(mine, 64, 1) * sign_of
            stacked.append(jnp.concatenate([mine, turned], axis=0))
        third = dot((tz[0], tz[1]), split(jnp.concatenate(stacked, axis=1)))
        for n in range(2):
            value = third[:, 128 * n : 128 * n + 128]
            add_bins(k, 2 * pair + n, value * value * weight)

    for k in range(LIVE_DEV):

        def arrive(turn, carry):
            mode_copy(k, turn, (ring + gzs - turn) % gzs).wait_recv()
            mode_copy(k, turn, ring).wait_send()
            return carry

        def middle(part_at, carry):
            forward(2, 2 * k + part_at)

            def go(pair, c):
                pair_modes(k, part_at * (per // 4) + pair)
                return c

            lax.fori_loop(0, per // 4, go, 0)
            return carry

        lax.fori_loop(1, gzs, arrive, 0)
        modes[k][pl.ds(ring * depth, depth)] = sent[k][ring]
        lax.fori_loop(0, 2, middle, 0)
    forward(2, jnp.int32(PIECES))

    at_lane = lax.broadcasted_iota(jnp.int32, (NBINS, 128), 1)
    at_row = lax.broadcasted_iota(jnp.int32, (NBINS, 128), 0)
    rows = []
    for k in range(LIVE_DEV + 1):
        summed = jnp.sum(jnp.sum(acc[k], axis=1), axis=1, keepdims=True)
        rows.append(jnp.sum(jnp.where(at_lane == at_row, summed, 0.0), axis=0, keepdims=True))
    own_part[...] = jnp.concatenate(rows + [jnp.zeros((8 - LIVE_DEV - 1, 128), jnp.float32)], axis=0)

    def part_copy(turn, to):
        return pltpu.make_async_remote_copy(
            src_ref=own_part, dst_ref=part.at[to],
            send_sem=part_send.at[turn], recv_sem=part_recv.at[turn],
            device_id=(me, (ring + turn) % gzs), device_id_type=MESH,
        )

    def part_start(turn, carry):
        part_copy(turn, ring).start()
        return carry

    def part_wait(turn, carry):
        part_copy(turn, (ring + gzs - turn) % gzs).wait_recv()
        part_copy(turn, ring).wait_send()
        return carry

    lax.fori_loop(1, gzs, part_start, 0)

    total = jnp.int32(0)
    slots = [jnp.int32(0)] * rep_dev

    def position_of(p, found):
        slot = dest[p]
        return tuple(jnp.where(slot == me * rep_dev + j, p, found[j]) for j in range(rep_dev))

    found = lax.fori_loop(0, reps * rep_dev, position_of, tuple(slots))

    def look(i, state):
        total, rank, owners, ranks = state
        number = counts[i]
        rank = jnp.where(i % rep_dev == 0, 0, rank)
        ends = total + number
        hits = [(found[j] >= total) & (found[j] < ends) for j in range(rep_dev)]
        owners = tuple(jnp.where(hits[j], i // rep_dev, owners[j]) for j in range(rep_dev))
        ranks = tuple(jnp.where(hits[j], rank, ranks[j]) for j in range(rep_dev))
        return ends, rank + (number > 0).astype(jnp.int32), owners, ranks

    _, _, owners, ranks = lax.fori_loop(
        0, reps * rep_dev, look, (total, jnp.int32(0), tuple(slots), tuple(slots))
    )

    lax.fori_loop(1, gzs, part_wait, 0)
    part[ring] = own_part[...]
    binned = jnp.sum(part[...], axis=0)
    whole = binned[LIVE_DEV : LIVE_DEV + 1]
    used = lax.broadcasted_iota(jnp.int32, (8, 128), 1) < NBINS
    own_prop[...] = jnp.where(used, binned / jnp.where(used, float(L**3) * whole, 1.0), 0.0)

    def prop_copy(turn, to):
        return pltpu.make_async_remote_copy(
            src_ref=own_prop, dst_ref=props.at[to],
            send_sem=prop_send.at[turn], recv_sem=prop_recv.at[turn],
            device_id=((me + turn) % reps, ring), device_id_type=MESH,
        )

    def prop_start(turn, carry):
        prop_copy(turn, me).start()
        return carry

    def prop_wait(turn, carry):
        prop_copy(turn, (me + reps - turn) % reps).wait_recv()
        prop_copy(turn, me).wait_send()
        return carry

    lax.fori_loop(1, reps, prop_start, 0)

    def late(step, carry):
        forward(3 + step // (PIECES + 1), step % (PIECES + 1))
        return carry

    lax.fori_loop(0, (levels - 3) * (PIECES + 1), late, 0)

    lax.fori_loop(1, reps, prop_wait, 0)
    props[me] = own_prop[...]
    for j in range(rep_dev):
        prop[j : j + 1, :] = props[owners[j], pl.ds(ranks[j], 1), :][:, :NBINS]

    for k in range(LIVE_DEV):
        keep(k).wait()

    def from_mate(step, carry):
        origin, index = step // PIECES, step % PIECES

        @pl.when(index > 0)
        def _():
            send(origin * COLUMNS + 1 - x, index, own_x_sem.at[index], mate).wait_recv()

        return carry

    lax.fori_loop(0, levels * PIECES, from_mate, 0)

    for j in range(rep_dev):
        chosen[j] = owners[j] * LIVE_DEV + ranks[j]

    def drain(index, carry):
        send(me, index, own_x_sem.at[index], mate).wait_send()
        for origin, x_sem, last in ((0, up_x_sem, levels - 1), (levels - 1, down_x_sem, 0)):

            @pl.when((z == last) & (index > 0))
            def _():
                send(origin * COLUMNS + x, index, x_sem.at[index], mate).wait_send()

        return carry

    lax.fori_loop(0, PIECES, drain, 0)


def local(lattice_field, langevin_noise, masses, counts, dest_slots, mode_bins):
    rep_dev, depth, sites = lattice_field.shape
    reps, gzs = lax.axis_size("rep"), lax.axis_size("gz")
    per = L // gzs
    levels = reps // COLUMNS
    assert levels >= 4
    f32, dma = jnp.float32, pltpu.SemaphoreType.DMA
    scratch = [
        pltpu.VMEM((SWEEPS * LIVE_DEV, depth + 16, sites), f32),
        *[pltpu.VMEM((rep_dev, depth, sites), f32)] * SWEEPS,
        *[pltpu.VMEM((2, depth, sites // 2), f32)] * LIVE_DEV,
        pltpu.VMEM((SWEEPS, 2, LIVE_DEV, 1, sites), f32),
        pltpu.VMEM((SWEEPS, 2, LIVE_DEV, 1, sites), f32),
        pltpu.VMEM((LIVE_DEV, depth * CHUNKS, 128), f32),
        *[pltpu.VMEM((gzs, depth, per, 128), f32)] * LIVE_DEV,
        *[pltpu.VMEM((L, per, 128), f32)] * LIVE_DEV,
        pltpu.VMEM((per, L, 128), jnp.int32),
        pltpu.VMEM((LIVE_DEV + 1, NBINS, 8, 128), f32),
        pltpu.VMEM((gzs, 8, 128), f32),
        pltpu.VMEM((reps, 8, 128), f32),
        pltpu.VMEM((8, 128), f32),
        pltpu.VMEM((8, 128), f32),
        dma((PIECES + 1,)),
        dma((PIECES + 1,)),
        dma((PIECES,)),
        dma((PIECES,)),
        dma((PIECES,)),
        dma((reps * PIECES,)),
        dma((SWEEPS, 2, LIVE_DEV)),
        dma((SWEEPS, 2, LIVE_DEV)),
        dma((LIVE_DEV * gzs,)),
        dma((LIVE_DEV * gzs,)),
        dma((gzs,)),
        dma((gzs,)),
        dma((reps,)),
        dma((reps,)),
        dma((SWEEPS,)),
        dma((LIVE_DEV,)),
    ]
    smem = pl.BlockSpec(memory_space=pltpu.SMEM)
    vmem = pl.BlockSpec(memory_space=pltpu.VMEM)
    hbm = pl.BlockSpec(memory_space=pl.ANY)
    gathered, chosen, propagator = pl.pallas_call(
        functools.partial(kernel, reps, gzs, rep_dev),
        out_shape=(
            jax.ShapeDtypeStruct((reps * LIVE_DEV, 2, depth, sites // 2), f32),
            jax.ShapeDtypeStruct((rep_dev,), jnp.int32),
            jax.ShapeDtypeStruct((rep_dev, NBINS), f32),
        ),
        in_specs=[smem, smem, vmem, hbm, vmem, vmem, vmem, vmem, vmem],
        out_specs=(hbm, smem, vmem),
        scratch_shapes=scratch,
        compiler_params=pltpu.CompilerParams(
            collective_id=0, has_side_effects=True, vmem_limit_bytes=56 * 1024 * 1024
        ),
    )(
        counts, dest_slots, lattice_field, langevin_noise, masses,
        jnp.transpose(mode_bins, (2, 0, 1)), *map(jnp.asarray, tables()),
    )
    return pl.pallas_call(
        pick,
        out_shape=(
            jax.ShapeDtypeStruct(lattice_field.shape, f32),
            jax.ShapeDtypeStruct((rep_dev, NBINS), f32),
        ),
        in_specs=[smem, hbm, hbm],
        out_specs=(hbm, hbm),
        scratch_shapes=[dma((2 * rep_dev + 1,))],
        compiler_params=pltpu.CompilerParams(vmem_limit_bytes=56 * 1024 * 1024),
    )(chosen, gathered, propagator)


def pick(chosen, gathered, prop, out, prop_out, sem):
    rep_dev, half = out.shape[0], gathered.shape[3]
    copies = [pltpu.make_async_copy(prop, prop_out, sem.at[2 * rep_dev])]
    for j in range(rep_dev):
        for h in range(2):
            target = out.at[j, :, half * h : half * h + half]
            copies.append(pltpu.make_async_copy(gathered.at[chosen[j], h], target, sem.at[2 * j + h]))
    for copy in copies:
        copy.start()
    for copy in copies:
        copy.wait()


def solution(mesh):
    in_specs = (
        P("rep", "gz", None),
        P(None, "rep", "gz", None),
        P("gz", None),
        P(),
        P(),
        P("gz", None, None),
    )
    out_specs = (P("rep", "gz", None), P("rep", None))
    return jax.shard_map(local, mesh=mesh, in_specs=in_specs, out_specs=out_specs, check_vma=False)
```

```python
import functools

import jax
import jax.numpy as jnp
import numpy as np
from jax import lax
from jax.experimental import pallas as pl
from jax.experimental.pallas import tpu as pltpu
from jax.sharding import PartitionSpec as P

L = 64
HALF = L // 2 + 1
SWEEPS = 2
NBINS = 16
LIVE_DEV = 3
COLUMNS = 2
PIECES = 2 * LIVE_DEV
CHUNKS = L * L // 128

step_size = 0.1
quartic = 0.5
kick = float(np.sqrt(np.float32(2.0 * step_size)))
MESH = pl.DeviceIdType.MESH


def tables():
    angle = 2.0 * np.pi / L * (np.outer(np.arange(L), np.arange(L)) % L)
    cos, sin = np.cos(angle), np.sin(angle)
    along_x = np.zeros((128, 512))
    for parity in range(2):
        rows = slice(64 * parity, 64 * parity + 64)
        at = 128 * parity
        along_x[rows, at : at + HALF] = cos[:, :HALF]
        along_x[rows, at + 64 : at + 64 + HALF] = -sin[:, :HALF]
        at = 256 + 128 * parity
        along_x[rows, at : at + HALF] = -sin[:, :HALF]
        along_x[rows, at + 64 : at + 64 + HALF] = -cos[:, :HALF]
    along_y = np.concatenate([cos[:, 0::2], cos[:, 1::2], sin[:, 0::2], sin[:, 1::2]], axis=1)
    along_z = np.concatenate([cos, sin], axis=1)

    def halves(table):
        table = table.astype(np.float32)
        high = table.astype(jnp.bfloat16)
        return np.stack([high, (table - high.astype(np.float32)).astype(jnp.bfloat16)])

    return halves(along_x), halves(along_y), halves(along_z)


def split(value):
    high = value.astype(jnp.bfloat16)
    return high, (value - high.astype(jnp.float32)).astype(jnp.bfloat16)


def dot(left, right):
    def one(a, b):
        return jnp.dot(a, b, preferred_element_type=jnp.float32)

    return one(left[0], right[0]) + (one(left[0], right[1]) + one(left[1], right[0]))


def kernel(reps, gzs, rep_dev, counts, dest, field, noise_in, masses, bins_in, tx, ty, tz, gathered, chosen, prop, *scratch):
    (
        swept, noise0, noise1, own0, own1, own2, edge_out, edge_in, work, sent0, sent1, sent2, modes0, modes1, modes2, bins, acc, part, props, own_part, own_prop,
        up_sem, down_sem, own_x_sem, up_x_sem, down_x_sem, recv_sem,
        edge_send, edge_recv, mode_send, mode_recv, part_send, part_recv, prop_send, prop_recv, noise_sem, keep_sem,
    ) = scratch
    own, noise = (own0, own1, own2), (noise0, noise1)
    sent, modes = (sent0, sent1, sent2), (modes0, modes1, modes2)
    depth = field.shape[1]
    per = L // gzs
    levels = reps // COLUMNS
    me, ring = lax.axis_index("rep"), lax.axis_index("gz")
    z, x = me // COLUMNS, me % COLUMNS
    mate = z * COLUMNS + (1 - x)

    barrier = pltpu.get_barrier_semaphore()

    def greet(turn, carry):
        pl.semaphore_signal(barrier, inc=1, device_id=(me, (ring + turn) % gzs), device_id_type=MESH)
        return carry

    def greet_rep(turn, carry):
        pl.semaphore_signal(barrier, inc=1, device_id=((me + turn) % reps, ring), device_id_type=MESH)
        return carry

    lax.fori_loop(1, gzs, greet, 0)
    lax.fori_loop(1, reps, greet_rep, 0)

    def noise_copy(turn):
        return pltpu.make_async_copy(noise_in.at[turn], noise[turn], noise_sem.at[turn])

    for turn in range(SWEEPS):
        noise_copy(turn).start()

    live = [jnp.int32(0)] * LIVE_DEV
    rank = jnp.int32(0)
    for i in range(rep_dev):
        alive = counts[me * rep_dev + i] > 0
        live = [jnp.where(alive & (rank == k), i, live[k]) for k in range(LIVE_DEV)]
        rank = rank + alive.astype(jnp.int32)

    lane = lax.broadcasted_iota(jnp.int32, (depth, 128), 1)
    first_x, last_x, even_y = lane % 64 == 0, lane % 64 == 63, lane < 64

    def send_own(index, sem, target):
        return pltpu.make_async_remote_copy(
            src_ref=own[index // 2].at[index % 2], dst_ref=piece(me, index), send_sem=sem,
            recv_sem=recv_sem.at[me * PIECES + index], device_id=(target, ring), device_id_type=MESH,
        )

    def edge_copy(turn, side, k):
        target = (ring + 1) % gzs if side == 0 else (ring + gzs - 1) % gzs
        return pltpu.make_async_remote_copy(
            src_ref=edge_out.at[turn, side, k], dst_ref=edge_in.at[turn, side, k],
            send_sem=edge_send.at[turn, side, k], recv_sem=edge_recv.at[turn, side, k],
            device_id=(me, target), device_id_type=MESH,
        )

    def edge_rows(turn, k):
        edge_out[turn, 0, k] = swept[turn * LIVE_DEV + k, 8 + depth - 1 : 8 + depth, :]
        edge_out[turn, 1, k] = swept[turn * LIVE_DEV + k, 8:9, :]

    def edge_start(turn, k):
        for side in range(2):
            edge_copy(turn, side, k).start()

    def edge_wait(turn, k):
        for side in range(2):
            edge_copy(turn, side, k).wait()
        swept[turn * LIVE_DEV + k, 7:8, :] = edge_in[turn, 0, k]
        swept[turn * LIVE_DEV + k, 8 + depth : 9 + depth, :] = edge_in[turn, 1, k]

    def piece(owner, index):
        return gathered.at[owner * LIVE_DEV + index // 2, index % 2]

    def send(owner, index, sem, target):
        ref = piece(owner, index)
        return pltpu.make_async_remote_copy(
            src_ref=ref, dst_ref=ref, send_sem=sem, recv_sem=recv_sem.at[owner * PIECES + index],
            device_id=(target, ring), device_id_type=MESH,
        )

    for k in range(LIVE_DEV):
        swept[k, 8 : 8 + depth, :] = field[live[k]]
        edge_rows(0, k)
    pl.semaphore_wait(barrier, gzs - 1 + reps - 1)
    for k in range(LIVE_DEV):
        edge_start(0, k)

    narrow = lax.broadcasted_iota(jnp.int32, (per, 128), 1) % 64 < HALF
    for kz in range(HALF):
        mine = bins_in[kz]
        mine = jnp.where(narrow, jnp.concatenate([mine, mine], axis=1), -1)
        bins[:, kz, :] = mine
        if 0 < kz < L // 2:
            bins[:, L - kz, :] = mine
    acc[...] = jnp.zeros(acc.shape, jnp.float32)
    wide = lax.broadcasted_iota(jnp.int32, (L, 128), 1)
    wave_x = wide % 64
    weight = jnp.where((wave_x == 0) | (wave_x == L // 2), 1.0, 2.0).astype(jnp.float32)
    sign_of = jnp.where(wide < 64, 1.0, -1.0).astype(jnp.float32)
    real_weight = jnp.where(wide < 64, weight, 0.0)

    def add_bins(k, q, value):
        here = bins[q]
        for b in range(NBINS):
            taken = jnp.where(here == b, value, 0.0)
            acc[k, b] += jnp.sum(taken.reshape(L // 8, 8, 128), axis=0)

    def weigh(q, carry):
        add_bins(LIVE_DEV, q, real_weight)
        return carry

    lax.fori_loop(0, per, weigh, 0)

    def keep(k):
        return pltpu.make_async_copy(own[k], gathered.at[me * LIVE_DEV + k], keep_sem.at[k])

    def sweep(turn, k):
        edge_wait(turn, k)
        from_at, to_at = turn * LIVE_DEV + k, (turn + 1) * LIVE_DEV + k

        def block(j, carry):
            def lanes(at):
                return pl.ds(pl.multiple_of(at % CHUNKS * 128, 128), 128)

            here = lanes(j)
            center = swept[from_at, 8 : 8 + depth, here]
            before = pltpu.roll(swept[from_at, 8 : 8 + depth, lanes(j + CHUNKS - 1)], 64, 1)
            after = pltpu.roll(swept[from_at, 8 : 8 + depth, lanes(j + 1)], 64, 1)
            beside = swept[from_at, 7 : 7 + depth, here] + swept[from_at, 9 : 9 + depth, here]
            beside += pltpu.roll(center, 64, 1) + jnp.where(even_y, before, after)
            beside += jnp.where(first_x, pltpu.roll(center, 65, 1), pltpu.roll(center, 1, 1))
            beside += jnp.where(last_x, pltpu.roll(center, 63, 1), pltpu.roll(center, 127, 1))
            drift = 6.0 * center - beside + masses[:, here] * center + quartic * center * center * center
            fresh = center - step_size * drift + kick * noise[turn][live[k], :, here]
            if turn + 1 < SWEEPS:
                swept[to_at, 8 : 8 + depth, here] = fresh
            else:
                at = pl.ds(pl.multiple_of(j % (CHUNKS // 2) * 128, 128), 128)
                own[k][j // (CHUNKS // 2), :, at] = fresh
                work[k, pl.ds(j, depth, stride=CHUNKS), :] = fresh
            return carry

        if turn + 1 < SWEEPS:
            lax.fori_loop(0, CHUNKS, block, 0, unroll=8)
            edge_rows(turn + 1, k)
            edge_start(turn + 1, k)
            return
        for h in range(2):
            lax.fori_loop(h * CHUNKS // 2, (h + 1) * CHUNKS // 2, block, 0, unroll=8)
            index = 2 * k + h
            send_own(index, own_x_sem.at[index], mate).start()

            @pl.when(z + 1 < levels)
            def _():
                send_own(index, up_sem.at[index], me + COLUMNS).start()

            @pl.when(z > 0)
            def _():
                send_own(index, down_sem.at[index], me - COLUMNS).start()

        keep(k).start()

    noise_copy(0).wait()
    sweep(0, 0)
    noise_copy(1).wait()
    for k in range(1, LIVE_DEV):
        sweep(0, k)
        sweep(1, k - 1)
    sweep(1, LIVE_DEV - 1)

    send(mate, 0, own_x_sem.at[0], mate).wait_recv()

    @pl.when(z + 1 < levels)
    def _():
        send(mate, 0, up_sem.at[PIECES], me + COLUMNS).start()

    @pl.when(z > 0)
    def _():
        send(mate, 0, down_sem.at[PIECES], me - COLUMNS).start()

    def forward(t, at):
        foreign = (at == PIECES).astype(jnp.int32)
        index = at - PIECES * foreign
        column = x + foreign * (1 - 2 * x)
        for sign, sem, x_sem, edge in ((1, up_sem, up_x_sem, levels - 1), (-1, down_sem, down_x_sem, 0)):
            origin = z - sign * t
            owner = origin * COLUMNS + column
            before = (origin + sign) * COLUMNS + column

            @pl.when((origin >= 0) & (origin < levels))
            def _():
                send(owner, index, sem.at[at], mate).wait_recv()

            @pl.when((origin + sign >= 0) & (origin + sign < levels) & (z != edge))
            def _():
                send(before, index, sem.at[at], me + sign * COLUMNS).wait_send()

            @pl.when((origin >= 0) & (origin < levels) & (z != edge))
            def _():
                send(owner, index, sem.at[at], me + sign * COLUMNS).start()

            @pl.when((t > 1) & (origin + sign >= 0) & (origin + sign < levels) & (at < PIECES) & (at > 0))
            def _():
                send(before, index, x_sem.at[index], mate).wait_send()

            @pl.when((origin >= 0) & (origin < levels) & (at < PIECES) & (at > 0))
            def _():
                send(owner, index, x_sem.at[index], mate).start()

    half_depth = depth // 2

    def planes(k, part_at):
        rows = half_depth * CHUNKS
        value = work[k, pl.ds(pl.multiple_of(part_at * rows, rows), rows), :]
        first = dot(split(value), (tx[0], tx[1]))
        for pair in range(half_depth // 2):
            stacked = []
            for plane in (2 * pair, 2 * pair + 1):
                mine = first[plane * CHUNKS : (plane + 1) * CHUNKS]
                stacked.append(jnp.concatenate([mine[:, 128 * c : 128 * c + 128] for c in range(4)], axis=0))
            second = dot((ty[0], ty[1]), split(jnp.concatenate(stacked, axis=1)))
            for d in range(gzs):
                rows = second[d * per : (d + 1) * per]
                at = part_at * half_depth + 2 * pair
                sent[k][d, at] = rows[:, :128]
                sent[k][d, at + 1] = rows[:, 128:]

    def mode_copy(k, turn, source):
        target = (ring + turn) % gzs
        return pltpu.make_async_remote_copy(
            src_ref=sent[k].at[target],
            dst_ref=modes[k].at[pl.ds(source * depth, depth)],
            send_sem=mode_send.at[k * gzs + turn],
            recv_sem=mode_recv.at[k * gzs + turn],
            device_id=(me, target), device_id_type=MESH,
        )

    def send_modes(k):

        def one(turn, carry):
            mode_copy(k, turn, ring).start()
            return carry

        lax.fori_loop(1, gzs, one, 0)

    for k in range(LIVE_DEV):

        def early(part_at, carry):
            forward(1, 2 * k + part_at)
            planes(k, part_at)
            return carry

        lax.fori_loop(0, 2, early, 0)
        send_modes(k)
    forward(1, jnp.int32(PIECES))

    def pair_modes(k, pair):
        stacked = []
        for q in (2 * pair, 2 * pair + 1):
            mine = modes[k][:, q, :]
            turned = pltpu.roll(mine, 64, 1) * sign_of
            stacked.append(jnp.concatenate([mine, turned], axis=0))
        third = dot((tz[0], tz[1]), split(jnp.concatenate(stacked, axis=1)))
        for n in range(2):
            value = third[:, 128 * n : 128 * n + 128]
            add_bins(k, 2 * pair + n, value * value * weight)

    for k in range(LIVE_DEV):

        def arrive(turn, carry):
            mode_copy(k, turn, (ring + gzs - turn) % gzs).wait_recv()
            mode_copy(k, turn, ring).wait_send()
            return carry

        def middle(part_at, carry):
            forward(2, 2 * k + part_at)

            def go(pair, c):
                pair_modes(k, part_at * (per // 4) + pair)
                return c

            lax.fori_loop(0, per // 4, go, 0)
            return carry

        lax.fori_loop(1, gzs, arrive, 0)
        modes[k][pl.ds(ring * depth, depth)] = sent[k][ring]
        lax.fori_loop(0, 2, middle, 0)
    forward(2, jnp.int32(PIECES))

    at_lane = lax.broadcasted_iota(jnp.int32, (NBINS, 128), 1)
    at_row = lax.broadcasted_iota(jnp.int32, (NBINS, 128), 0)
    rows = []
    for k in range(LIVE_DEV + 1):
        summed = jnp.sum(jnp.sum(acc[k], axis=1), axis=1, keepdims=True)
        rows.append(jnp.sum(jnp.where(at_lane == at_row, summed, 0.0), axis=0, keepdims=True))
    own_part[...] = jnp.concatenate(rows + [jnp.zeros((8 - LIVE_DEV - 1, 128), jnp.float32)], axis=0)

    def part_copy(turn, to):
        return pltpu.make_async_remote_copy(
            src_ref=own_part, dst_ref=part.at[to],
            send_sem=part_send.at[turn], recv_sem=part_recv.at[turn],
            device_id=(me, (ring + turn) % gzs), device_id_type=MESH,
        )

    def part_start(turn, carry):
        part_copy(turn, ring).start()
        return carry

    def part_wait(turn, carry):
        part_copy(turn, (ring + gzs - turn) % gzs).wait_recv()
        part_copy(turn, ring).wait_send()
        return carry

    lax.fori_loop(1, gzs, part_start, 0)

    total = jnp.int32(0)
    slots = [jnp.int32(0)] * rep_dev

    def position_of(p, found):
        slot = dest[p]
        return tuple(jnp.where(slot == me * rep_dev + j, p, found[j]) for j in range(rep_dev))

    found = lax.fori_loop(0, reps * rep_dev, position_of, tuple(slots))

    def look(i, state):
        total, rank, owners, ranks = state
        number = counts[i]
        rank = jnp.where(i % rep_dev == 0, 0, rank)
        ends = total + number
        hits = [(found[j] >= total) & (found[j] < ends) for j in range(rep_dev)]
        owners = tuple(jnp.where(hits[j], i // rep_dev, owners[j]) for j in range(rep_dev))
        ranks = tuple(jnp.where(hits[j], rank, ranks[j]) for j in range(rep_dev))
        return ends, rank + (number > 0).astype(jnp.int32), owners, ranks

    _, _, owners, ranks = lax.fori_loop(
        0, reps * rep_dev, look, (total, jnp.int32(0), tuple(slots), tuple(slots))
    )

    lax.fori_loop(1, gzs, part_wait, 0)
    part[ring] = own_part[...]
    binned = jnp.sum(part[...], axis=0)
    whole = binned[LIVE_DEV : LIVE_DEV + 1]
    used = lax.broadcasted_iota(jnp.int32, (8, 128), 1) < NBINS
    own_prop[...] = jnp.where(used, binned / jnp.where(used, float(L**3) * whole, 1.0), 0.0)

    def prop_copy(turn, to):
        return pltpu.make_async_remote_copy(
            src_ref=own_prop, dst_ref=props.at[to],
            send_sem=prop_send.at[turn], recv_sem=prop_recv.at[turn],
            device_id=((me + turn) % reps, ring), device_id_type=MESH,
        )

    def prop_start(turn, carry):
        prop_copy(turn, me).start()
        return carry

    def prop_wait(turn, carry):
        prop_copy(turn, (me + reps - turn) % reps).wait_recv()
        prop_copy(turn, me).wait_send()
        return carry

    lax.fori_loop(1, reps, prop_start, 0)

    def late(step, carry):
        forward(3 + step // (PIECES + 1), step % (PIECES + 1))
        return carry

    lax.fori_loop(0, (levels - 3) * (PIECES + 1), late, 0)

    lax.fori_loop(1, reps, prop_wait, 0)
    props[me] = own_prop[...]
    for j in range(rep_dev):
        prop[j : j + 1, :] = props[owners[j], pl.ds(ranks[j], 1), :][:, :NBINS]

    for k in range(LIVE_DEV):
        keep(k).wait()

    def from_mate(step, carry):
        origin, index = step // PIECES, step % PIECES

        @pl.when(index > 0)
        def _():
            send(origin * COLUMNS + 1 - x, index, own_x_sem.at[index], mate).wait_recv()

        return carry

    lax.fori_loop(0, levels * PIECES, from_mate, 0)

    for j in range(rep_dev):
        chosen[j] = owners[j] * LIVE_DEV + ranks[j]

    def drain(index, carry):
        send(me, index, own_x_sem.at[index], mate).wait_send()
        for origin, x_sem, last in ((0, up_x_sem, levels - 1), (levels - 1, down_x_sem, 0)):

            @pl.when((z == last) & (index > 0))
            def _():
                send(origin * COLUMNS + x, index, x_sem.at[index], mate).wait_send()

        return carry

    lax.fori_loop(0, PIECES, drain, 0)


def local(lattice_field, langevin_noise, masses, counts, dest_slots, mode_bins):
    rep_dev, depth, sites = lattice_field.shape
    reps, gzs = lax.axis_size("rep"), lax.axis_size("gz")
    per = L // gzs
    levels = reps // COLUMNS
    assert levels >= 4
    f32, dma = jnp.float32, pltpu.SemaphoreType.DMA
    scratch = [
        pltpu.VMEM((SWEEPS * LIVE_DEV, depth + 16, sites), f32),
        *[pltpu.VMEM((rep_dev, depth, sites), f32)] * SWEEPS,
        *[pltpu.VMEM((2, depth, sites // 2), f32)] * LIVE_DEV,
        pltpu.VMEM((SWEEPS, 2, LIVE_DEV, 1, sites), f32),
        pltpu.VMEM((SWEEPS, 2, LIVE_DEV, 1, sites), f32),
        pltpu.VMEM((LIVE_DEV, depth * CHUNKS, 128), f32),
        *[pltpu.VMEM((gzs, depth, per, 128), f32)] * LIVE_DEV,
        *[pltpu.VMEM((L, per, 128), f32)] * LIVE_DEV,
        pltpu.VMEM((per, L, 128), jnp.int32),
        pltpu.VMEM((LIVE_DEV + 1, NBINS, 8, 128), f32),
        pltpu.VMEM((gzs, 8, 128), f32),
        pltpu.VMEM((reps, 8, 128), f32),
        pltpu.VMEM((8, 128), f32),
        pltpu.VMEM((8, 128), f32),
        dma((PIECES + 1,)),
        dma((PIECES + 1,)),
        dma((PIECES,)),
        dma((PIECES,)),
        dma((PIECES,)),
        dma((reps * PIECES,)),
        dma((SWEEPS, 2, LIVE_DEV)),
        dma((SWEEPS, 2, LIVE_DEV)),
        dma((LIVE_DEV * gzs,)),
        dma((LIVE_DEV * gzs,)),
        dma((gzs,)),
        dma((gzs,)),
        dma((reps,)),
        dma((reps,)),
        dma((SWEEPS,)),
        dma((LIVE_DEV,)),
    ]
    smem = pl.BlockSpec(memory_space=pltpu.SMEM)
    vmem = pl.BlockSpec(memory_space=pltpu.VMEM)
    hbm = pl.BlockSpec(memory_space=pl.ANY)
    gathered, chosen, propagator = pl.pallas_call(
        functools.partial(kernel, reps, gzs, rep_dev),
        out_shape=(
            jax.ShapeDtypeStruct((reps * LIVE_DEV, 2, depth, sites // 2), f32),
            jax.ShapeDtypeStruct((rep_dev,), jnp.int32),
            jax.ShapeDtypeStruct((rep_dev, NBINS), f32),
        ),
        in_specs=[smem, smem, vmem, hbm, vmem, vmem, vmem, vmem, vmem],
        out_specs=(hbm, smem, vmem),
        scratch_shapes=scratch,
        compiler_params=pltpu.CompilerParams(
            collective_id=0, has_side_effects=True, vmem_limit_bytes=56 * 1024 * 1024
        ),
    )(
        counts, dest_slots, lattice_field, langevin_noise, masses,
        jnp.transpose(mode_bins, (2, 0, 1)), *map(jnp.asarray, tables()),
    )
    return pl.pallas_call(
        pick,
        out_shape=(
            jax.ShapeDtypeStruct(lattice_field.shape, f32),
            jax.ShapeDtypeStruct((rep_dev, NBINS), f32),
        ),
        in_specs=[smem, hbm, hbm],
        out_specs=(hbm, hbm),
        scratch_shapes=[
            pltpu.VMEM((rep_dev, 2, depth, sites // 2), f32),
            pltpu.VMEM((rep_dev, NBINS), f32),
            dma((2 * rep_dev + 1,)),
            dma((2 * rep_dev + 1,)),
        ],
        compiler_params=pltpu.CompilerParams(vmem_limit_bytes=56 * 1024 * 1024),
    )(chosen, gathered, propagator)


def pick(chosen, gathered, prop, out, prop_out, held, held_prop, in_sem, out_sem):
    rep_dev, half = out.shape[0], gathered.shape[3]
    loads = [pltpu.make_async_copy(prop, held_prop, in_sem.at[2 * rep_dev])]
    stores = [pltpu.make_async_copy(held_prop, prop_out, out_sem.at[2 * rep_dev])]
    for j in range(rep_dev):
        for h in range(2):
            lanes, at = slice(half * h, half * h + half), 2 * j + h
            loads.append(pltpu.make_async_copy(gathered.at[chosen[j], h], held.at[j, h], in_sem.at[at]))
            stores.append(pltpu.make_async_copy(held.at[j, h], out.at[j, :, lanes], out_sem.at[at]))
    for load in loads:
        load.start()
    for load, store in zip(loads, stores):
        load.wait()
        store.start()
    for store in stores:
        store.wait()


def solution(mesh):
    in_specs = (
        P("rep", "gz", None),
        P(None, "rep", "gz", None),
        P("gz", None),
        P(),
        P(),
        P("gz", None, None),
    )
    out_specs = (P("rep", "gz", None), P("rep", None))
    return jax.shard_map(local, mesh=mesh, in_specs=in_specs, out_specs=out_specs, check_vma=False)
```
